256 devices in a mesh: gx: 16 (over z, x_lo), mode: 16 (over y, x_hi, core).
Axes of the slice: x: 4 (x_hi: 2, x_lo: 2; x = x_hi * 2 + x_lo), y: 4, z: 8, core: 2. Of those that a mesh axis runs over, the one named last changes fastest.
Arguments:
- section_field: bfloat16 [1024, 2, 64, 4, 128], P('mode', None, 'gx'), may hold values from -6 to 6
- base_field: bfloat16 [1024, 2, 64, 4, 128], P('mode', None, 'gx'), may hold values from -6 to 6
- prev_rate: float32 [1024, 2, 64, 4, 128], P('mode', None, 'gx'), may hold values from -6 to 6
- block_list: int32 [16, 5], P('mode'), may hold values from 0 to 15, as said below
- coupling: bfloat16 [16, 5, 5, 64, 64], P('mode'), may hold values from -0.3125 to 0.3125
- diffusivity: float32 [2], replicated, may hold values from 0.05 to 0.25
- reaction_fields: bfloat16 [4, 64, 4, 128], P(None, 'gx'), may hold values from -2 to 2
- species_mix: float32 [2, 2], replicated, may hold values from -1 to 1
Outputs:
- rate: float32 [1024, 2, 64, 4, 128], P('mode', None, 'gx')
- next_field: bfloat16 [1024, 2, 64, 4, 128], P('mode', None, 'gx')
The draws below stay inside these ranges and needn't reach their ends.
Inputs may be any that keep to these rules, and one draw needn't show every extreme that they name: `block_list`: row i lists block i first, then 5 - 2 other different blocks, each at a cyclic distance of 1 to 2 from i, then block (i + 8) modulo 16.
All inputs are finite; a program needn't handle non-finite values.
Results may differ from the reference program's by a relative error of at most 0.0022.
Values may be sent and summed in bfloat16 or wider, within the bound.
A program may use at most 64 MiB of HBM per device.

```python
import jax
import jax.numpy as jnp
from jax import lax

MB = 64
NBLK = 16
M = 1024
S = 2
K = 4
REACH = 2
NNZ = 5
NY = 4
NZ = 128
NX = 64


def draw_block_list(key, part):
    key = jax.random.fold_in(key, 3)
    dropped = jax.random.randint(key, (NBLK, 1), 0, 2 * REACH, dtype=jnp.int32)
    columns = jnp.arange(2 * REACH - 1, dtype=jnp.int32)[None, :]
    picked = columns + (columns >= dropped).astype(jnp.int32)
    offsets = jnp.where(picked < REACH, picked - REACH, picked - REACH + 1)
    row_index = jnp.arange(NBLK, dtype=jnp.int32)[:, None]
    others = (row_index + offsets + NBLK) % NBLK
    across = (row_index + NBLK // 2) % NBLK
    return jnp.concatenate([row_index, others, across], axis=1).astype(jnp.int32)


def shard_levels(key, extent, pieces, low, largest):
    def one(dim, blocks):
        heights = jax.random.uniform(jax.random.fold_in(jax.random.fold_in(key, 6), dim), (blocks,), jnp.float32, low / len(pieces), largest / len(pieces))
        return jnp.repeat(jnp.exp(heights), extent[dim] // blocks).reshape((-1,) + (1,) * (len(extent) - dim - 1))

    gain = one(*pieces[0])
    for cut in pieces[1:]:
        gain = gain * one(*cut)
    return gain


def scatter_about(stream_key, shape, scale, reach, cuts=(), held_as=jnp.bfloat16):
    values = jax.random.normal(stream_key, shape, jnp.float32) * scale
    if len(cuts) > 0:
        values = shard_levels(stream_key, shape, cuts, -0.22, 0.18) * values
    return jnp.clip(values, min=-reach, max=reach).astype(held_as)


def setup_inputs(seed: int = 0) -> dict:
    arg_keys = jax.random.split(jax.random.key(seed), 9)
    return {
        "section_field": scatter_about(arg_keys[0], (M, S, NX, NY, NZ), 1.0, 6.0, ((0, 16), (2, 16))),
        "base_field": scatter_about(arg_keys[1], (M, S, NX, NY, NZ), 1.0, 6.0, ((0, 16), (2, 16))),
        "prev_rate": scatter_about(arg_keys[2], (M, S, NX, NY, NZ), 1.0, 6.0, ((0, 16), (2, 16)), jnp.float32),
        "block_list": draw_block_list(jax.random.fold_in(arg_keys[8], 71), 0),
        "coupling": scatter_about(arg_keys[4], (NBLK, NNZ, 1 + K, MB, MB), (MB * NNZ) ** -0.5, 0.3125, ((0, 16),)),
        "diffusivity": jnp.clip(jax.random.uniform(arg_keys[5], (S,), jnp.float32, 0.05, 0.25), 0.05, 0.25),
        "reaction_fields": scatter_about(arg_keys[6], (K, NX, NY, NZ), 0.35, 2.0, ((1, 16),)),
        "species_mix": jnp.clip(jax.random.uniform(arg_keys[7], (S, S), jnp.float32, -1.0, 1.0), -1.0, 1.0),
    }


half_step = 0.25


def laplacian(field):
    values = field.astype(jnp.float32)
    total = -6.0 * values
    for axis_number in (2, 3, 4):
        total = total + jnp.roll(values, 1, axis_number) + jnp.roll(values, -1, axis_number)
    return total.astype(jnp.bfloat16)


def reference(section_field, base_field, prev_rate, block_list, coupling, diffusivity, reaction_fields, species_mix):
    grid_cells = NX * NY * NZ
    cells = S * grid_cells
    lap_blocks = laplacian(section_field).reshape(NBLK, MB, cells)
    field_blocks = section_field.reshape(NBLK, MB, cells)
    fields = reaction_fields.astype(jnp.float32).reshape(K, 1, grid_cells)
    fields = jnp.broadcast_to(fields, (K, S, grid_cells)).reshape(K, cells)

    def one_row(row):
        blocks = lax.dynamic_index_in_dim(block_list, row, 0, False)
        weights = lax.dynamic_index_in_dim(coupling, row, 0, False)

        def add_term(slot, state):
            diffusion, reaction = state
            index = lax.dynamic_index_in_dim(blocks, slot, 0, False).astype(jnp.int32)
            chosen = lax.dynamic_index_in_dim(weights, slot, 0, False)
            lap_block = lax.dynamic_index_in_dim(lap_blocks, index, 0, False)
            field_block = lax.dynamic_index_in_dim(field_blocks, index, 0, False)
            diffusion = diffusion + jnp.dot(chosen[0], lap_block, preferred_element_type=jnp.float32)
            for term in range(K):
                reaction = reaction + fields[term] * jnp.dot(chosen[1 + term], field_block, preferred_element_type=jnp.float32)
            return diffusion, reaction

        start_state = (jnp.zeros((MB, cells), jnp.float32), jnp.zeros((MB, cells), jnp.float32))
        return lax.fori_loop(0, NNZ, add_term, start_state)

    diffusion, reaction = lax.map(one_row, jnp.arange(NBLK, dtype=jnp.int32))
    diffusion = diffusion.reshape(M, S, NX, NY, NZ)
    reaction = reaction.reshape(M, S, NX, NY, NZ)
    current = section_field.astype(jnp.float32)
    mixed_parts = []
    for target in range(S):
        total = species_mix[target, 0] * current[:, 0]
        for source in range(1, S):
            total = total + species_mix[target, source] * current[:, source]
        mixed_parts.append(total)
    mixing = jnp.stack(mixed_parts, axis=1)
    rate = diffusivity[None, :, None, None, None] * diffusion - reaction + mixing
    next_field = (base_field.astype(jnp.float32) + half_step * (prev_rate + rate)).astype(jnp.bfloat16)
    return rate, next_field
```

```python
import jax
import jax.numpy as jnp
from jax import lax
from jax.sharding import PartitionSpec as P
import jax.experimental.pallas as pl
import jax.experimental.pallas.tpu as pltpu

MB = 64
NBLK = 16
K = 4
TERMS = 1 + K
NNZ = 5
MESH = pl.DeviceIdType.MESH

half_step = 0.25

OWN, SIB, ACROSS, CROSS, RELAY, SIB2 = range(6)
TRANSIT, HALO_LO, HALO_HI = 6, 7, 8
PLANES = (0, 3, 1, 2)
STRIDE = 32


def kernel(
    section_hbm,
    coupling_hbm,
    fields_hbm,
    blocks_ref,
    diffusivity_ref,
    mix_ref,
    out_ref,
    native,
    wide,
    couple,
    fields_in,
    fields,
    blocks,
    transit,
    weights,
    diff,
    react,
    edge,
    halo,
    local_sem,
    send_sem,
    recv_sem,
):
    g = lax.axis_index("gx")
    i = lax.axis_index("mode")
    y = i // 4
    h = lax.rem(i // 2, 2)
    c = lax.rem(i, 2)
    step = 1 - 2 * h

    def device(dy, hh, cc):
        return (g, lax.rem(y + dy + 4, 4) * 4 + hh * 2 + cc)

    at_cross = device(0, 1 - h, c)
    at_relay = device(step, h, c)
    at_back = device(-step, h, c)
    at_across = device(2, h, c)
    at_sib = device(0, h, 1 - c)
    at_up = (lax.rem(g + 1, 16), i)
    at_down = (lax.rem(g + 15, 16), i)

    load = pltpu.make_async_copy(section_hbm, native, local_sem.at[0])
    load.start()
    load_couple = pltpu.make_async_copy(coupling_hbm, couple, local_sem.at[1])
    load_couple.start()
    load_fields = pltpu.make_async_copy(fields_hbm, fields_in, local_sem.at[2])
    load_fields.start()

    barrier = pltpu.get_barrier_semaphore()
    for peer in (at_cross, at_relay, at_back, at_across, at_sib, at_up, at_down):
        pl.semaphore_signal(barrier, inc=1, device_id=peer, device_id_type=MESH)

    load.wait()

    @pl.loop(0, 8)
    def _(n):
        rows = pl.ds(pl.multiple_of(n * 256, 256), 256)
        wide[rows, :] = native[rows, :].astype(jnp.float32)

    for pos, plane in enumerate(PLANES):

        @pl.loop(0, 8)
        def _(sy, pos=pos, plane=plane):
            start = (sy // 4) * 16 + plane * 4 + lax.rem(sy, 4)
            blocks[OWN, pos, sy] = wide[pl.ds(start, MB, stride=STRIDE), :].astype(jnp.bfloat16)

    pl.semaphore_wait(barrier, 7)

    def send(kind, part, source, target, peer):
        return pltpu.make_async_remote_copy(
            src_ref=source,
            dst_ref=target,
            send_sem=send_sem.at[kind, part],
            recv_sem=recv_sem.at[kind, part],
            device_id=peer,
            device_id_type=MESH,
        )

    def part_of(slot, part):
        return blocks.at[slot, pl.ds(2 * part, 2)]

    def block_send(source, target, part, peer):
        return send(target, part, part_of(source, part), part_of(target, part), peer)

    cross = [block_send(OWN, CROSS, p, at_cross) for p in (0, 1)]
    relay = [block_send(CROSS, RELAY, p, at_relay) for p in (0, 1)]
    transit_send = send(TRANSIT, 1, part_of(OWN, 1), transit, at_back)
    across = [
        block_send(OWN, ACROSS, 0, at_across),
        send(ACROSS, 1, transit, part_of(ACROSS, 1), at_back),
    ]
    sib = send(SIB, 0, blocks.at[OWN], blocks.at[SIB], at_sib)
    sib_cross = [block_send(CROSS, SIB2, p, at_sib) for p in (0, 1)]
    sib_relay = [block_send(RELAY, SIB2, p, at_sib) for p in (0, 1)]
    halo_up = send(HALO_LO, 0, edge.at[1], halo.at[0], at_up)
    halo_down = send(HALO_HI, 0, edge.at[0], halo.at[1], at_down)

    cross[0].start()
    transit_send.start()
    across[0].start()
    cross[1].start()
    sib.start()

    load_couple.wait()
    load_fields.wait()
    fields[...] = fields_in[...].astype(jnp.float32)

    def chosen(target):
        target = lax.rem(target + NBLK, NBLK)
        total = None
        for n in range(1, NNZ - 1):
            keep = (blocks_ref[0, n] == target).astype(jnp.float32)
            term = keep * couple[n].astype(jnp.float32)
            total = term if total is None else total + term
        return total

    def side_by_side(first, second):
        pair = jnp.concatenate([first, second], axis=-1)
        return pair.reshape(TERMS * MB, 2 * MB).astype(jnp.bfloat16)

    weights[:, 0:128] = side_by_side(couple[0].astype(jnp.float32), chosen(i + 1 - 2 * c))
    weights[:, 128:256] = side_by_side(
        couple[NNZ - 1].astype(jnp.float32), chosen(i + 2 - 4 * h)
    )
    weights[:, 256:384] = side_by_side(chosen(i - 2 + 4 * h), chosen(i - 1 + 2 * c))

    def multiply(part, first, last, fresh):
        @pl.loop(0, 8)
        def _(n):
            at = n // 4
            plane = 3 * at if part == 0 else 1 + at
            sy = lax.rem(n, 4) * 2
            depth = (last - first) * MB
            sides = [
                blocks[first:last, 2 * part + at, sy + k].reshape(depth, 128) for k in (0, 1)
            ]
            result = jnp.dot(
                weights[:, first * MB : last * MB],
                jnp.concatenate(sides, axis=1),
                preferred_element_type=jnp.float32,
            )
            for k in (0, 1):
                columns = slice(128 * k, 128 * (k + 1))
                term_d = result[0:MB, columns]
                row = plane * 4 + lax.rem(sy + k, 4)
                term_r = fields[pl.ds(row, 1), :] * result[MB : 2 * MB, columns]
                for t in range(1, K):
                    term_r = term_r + fields[pl.ds(16 * t + row, 1), :] * result[
                        (1 + t) * MB : (2 + t) * MB, columns
                    ]
                if fresh:
                    diff[1 + plane, sy + k] = term_d
                    react[plane, sy + k] = term_r
                else:
                    total = diff[1 + plane, sy + k] + term_d
                    diff[1 + plane, sy + k] = total
                    react[plane, sy + k] += term_r
                    if part == 0:
                        edge[at, sy + k] = total.astype(jnp.bfloat16)

    def pass_on(copies, yes, part):
        @pl.when(yes)
        def _():
            copies[part].start()

    cross[0].wait_recv()
    relay[0].start()
    pass_on(sib_cross, c == h, 0)
    transit_send.wait_recv()
    across[1].start()
    sib.wait_recv()
    across[0].wait_recv()
    multiply(0, OWN, RELAY, True)
    cross[1].wait_recv()
    relay[1].start()
    pass_on(sib_cross, c == h, 1)
    relay[0].wait_recv()
    pass_on(sib_relay, c != h, 0)
    sib_cross[0].wait_recv()
    multiply(0, RELAY, SIB2 + 1, False)
    halo_up.start()
    halo_down.start()
    across[1].wait_recv()
    multiply(1, OWN, RELAY, True)
    relay[1].wait_recv()
    pass_on(sib_relay, c != h, 1)
    sib_cross[1].wait_recv()
    multiply(1, RELAY, SIB2 + 1, False)
    halo_up.wait_recv()
    halo_down.wait_recv()

    @pl.loop(0, 8)
    def _(sy):
        diff[0, sy] = halo[0, sy].astype(jnp.float32)
        diff[5, sy] = halo[1, sy].astype(jnp.float32)

    for pos, plane in enumerate(PLANES):

        @pl.loop(0, 8)
        def _(sy, pos=pos, plane=plane):
            s = sy // 4
            yy = lax.rem(sy, 4)
            center = diff[1 + plane, sy]
            lap = diff[plane, sy] + diff[2 + plane, sy]
            lap = lap + diff[1 + plane, s * 4 + lax.rem(yy + 1, 4)]
            lap = lap + diff[1 + plane, s * 4 + lax.rem(yy + 3, 4)]
            lap = lap + pltpu.roll(center, 1, 1) + pltpu.roll(center, 127, 1)
            lap = lap - 6.0 * center
            mixed = mix_ref[s, 0] * blocks[OWN, pos, yy].astype(jnp.float32)
            mixed = mixed + mix_ref[s, 1] * blocks[OWN, pos, 4 + yy].astype(jnp.float32)
            start = s * 16 + plane * 4 + yy
            out_ref[pl.ds(start, MB, stride=STRIDE), :] = (
                react[plane, sy] - diffusivity_ref[s] * lap - mixed
            )

    for copy in (*cross, *relay, transit_send, *across, sib, *sib_cross, halo_up, halo_down):
        copy.wait_send()


def shards(
    section_field,
    base_field,
    prev_rate,
    block_list,
    coupling,
    diffusivity,
    reaction_fields,
    species_mix,
):
    rows, species, planes, depth, width = section_field.shape
    flat = rows * species * planes * depth
    lines = species * depth
    anywhere = pl.BlockSpec(memory_space=pl.ANY)
    scalars = pl.BlockSpec(memory_space=pltpu.SMEM)
    minus_rate = pl.pallas_call(
        kernel,
        name="galerkin",
        out_shape=jax.ShapeDtypeStruct((flat, width), jnp.float32),
        in_specs=[anywhere, anywhere, anywhere, scalars, scalars, scalars],
        out_specs=pl.BlockSpec(memory_space=pltpu.VMEM),
        scratch_shapes=[
            pltpu.VMEM((flat, width), jnp.bfloat16),
            pltpu.VMEM((flat, width), jnp.float32),
            pltpu.VMEM((NNZ, TERMS, MB, MB), jnp.bfloat16),
            pltpu.VMEM((K * planes * depth, width), jnp.bfloat16),
            pltpu.VMEM((K * planes * depth, width), jnp.float32),
            pltpu.VMEM((6, planes, lines, MB, width), jnp.bfloat16),
            pltpu.VMEM((2, lines, MB, width), jnp.bfloat16),
            pltpu.VMEM((TERMS * MB, 6 * MB), jnp.bfloat16),
            pltpu.VMEM((planes + 2, lines, MB, width), jnp.float32),
            pltpu.VMEM((planes, lines, MB, width), jnp.float32),
            pltpu.VMEM((2, lines, MB, width), jnp.bfloat16),
            pltpu.VMEM((2, lines, MB, width), jnp.bfloat16),
            pltpu.SemaphoreType.DMA((3,)),
            pltpu.SemaphoreType.DMA((9, 2)),
            pltpu.SemaphoreType.DMA((9, 2)),
        ],
        compiler_params=pltpu.CompilerParams(
            collective_id=0, has_side_effects=True, vmem_limit_bytes=32 * 1024 * 1024
        ),
        cost_estimate=pl.CostEstimate(
            flops=2 * TERMS * 6 * MB * MB * species * planes * depth * width,
            bytes_accessed=2**21,
            transcendentals=0,
        ),
    )(
        section_field.reshape(flat, width),
        coupling.reshape(NNZ, TERMS, MB, MB),
        reaction_fields.reshape(K * planes * depth, width),
        block_list,
        diffusivity,
        species_mix,
    )
    rate = -minus_rate.reshape(section_field.shape)
    next_field = (base_field.astype(jnp.float32) + half_step * (prev_rate + rate)).astype(
        jnp.bfloat16
    )
    return (rate, next_field)


def solution(mesh):
    placed = (
        P("mode", None, "gx", None, None),
        P("mode", None, "gx", None, None),
        P("mode", None, "gx", None, None),
        P("mode", None),
        P("mode", None, None, None, None),
        P(),
        P(None, "gx", None, None),
        P(),
    )
    return jax.shard_map(
        shards,
        mesh=mesh,
        in_specs=placed,
        out_specs=(P("mode", None, "gx", None, None), P("mode", None, "gx", None, None)),
        check_vma=False,
    )
```

```python
import jax
import jax.numpy as jnp
from jax import lax
from jax.sharding import PartitionSpec as P
import jax.experimental.pallas as pl
import jax.experimental.pallas.tpu as pltpu

MB = 64
NBLK = 16
K = 4
TERMS = 1 + K
NNZ = 5
MESH = pl.DeviceIdType.MESH

half_step = 0.25

OWN, SIB, ACROSS, CROSS, RELAY, SIB2 = range(6)
TRANSIT, HALO_LO, HALO_HI = 6, 7, 8
PLANES = (0, 3, 1, 2)
STRIDE = 32


def kernel(
    section_hbm,
    coupling_hbm,
    fields_hbm,
    list_hbm,
    diffusivity_hbm,
    mix_hbm,
    base_hbm,
    prev_hbm,
    out_ref,
    held_ref,
    list_ref,
    diffusivity_ref,
    mix_ref,
    base,
    native,
    wide,
    couple,
    fields_in,
    fields,
    blocks,
    transit,
    weights,
    diff,
    react,
    edge,
    halo,
    local_sem,
    send_sem,
    recv_sem,
    ready_sem,
    slabs_sem,
):
    g = lax.axis_index("gx")
    i = lax.axis_index("mode")
    y = i // 4
    h = lax.rem(i // 2, 2)
    c = lax.rem(i, 2)
    step = 1 - 2 * h

    def device(dy, hh, cc):
        return (g, lax.rem(y + dy + 4, 4) * 4 + hh * 2 + cc)

    at_cross = device(0, 1 - h, c)
    at_relay = device(step, h, c)
    at_back = device(-step, h, c)
    at_across = device(2, h, c)
    at_sib = device(0, h, 1 - c)
    at_up = (lax.rem(g + 1, 16), i)
    at_down = (lax.rem(g + 15, 16), i)

    def signal(sem, peer):
        pl.semaphore_signal(sem, inc=1, device_id=peer, device_id_type=MESH)

    load = pltpu.make_async_copy(section_hbm, native, local_sem.at[0])
    load.start()
    loads = [
        pltpu.make_async_copy(source, target, local_sem.at[1 + n])
        for n, (source, target) in enumerate(
            (
                (coupling_hbm, couple),
                (fields_hbm, fields_in),
                (list_hbm, list_ref),
                (diffusivity_hbm, diffusivity_ref),
                (mix_hbm, mix_ref),
                (base_hbm, base),
                (prev_hbm, held_ref),
            )
        )
    ]

    barrier = pltpu.get_barrier_semaphore()
    for peer in (device(0, 1 - h, 0), device(1, h, 0), device(3, h, 0), device(2, h, 0)):
        signal(barrier, peer)

    @pl.when(c == 1)
    def _():
        signal(barrier, at_sib)

    for copy in loads:
        copy.start()

    load.wait()

    @pl.loop(0, 8)
    def _(n):
        rows = pl.ds(pl.multiple_of(n * 256, 256), 256)
        wide[rows, :] = native[rows, :].astype(jnp.float32)

    for pos, plane in enumerate(PLANES):

        @pl.loop(0, 8)
        def _(sy, pos=pos, plane=plane):
            start = (sy // 4) * 16 + plane * 4 + lax.rem(sy, 4)
            blocks[OWN, pos, sy] = wide[pl.ds(start, MB, stride=STRIDE), :].astype(jnp.bfloat16)

    @pl.when(c == 0)
    def _():
        pl.semaphore_wait(barrier, 9)
        signal(ready_sem, at_sib)

    @pl.when(c == 1)
    def _():
        pl.semaphore_wait(ready_sem, 1)
        signal(barrier, at_up)
        signal(barrier, at_down)

    def send(kind, part, source, target, peer):
        return pltpu.make_async_remote_copy(
            src_ref=source,
            dst_ref=target,
            send_sem=send_sem.at[kind, part],
            recv_sem=recv_sem.at[kind, part],
            device_id=peer,
            device_id_type=MESH,
        )

    def block_send(source, target, pos, peer):
        return send(target, pos, blocks.at[source, pos], blocks.at[target, pos], peer)

    every = range(4)
    cross = [block_send(OWN, CROSS, p, at_cross) for p in every]
    relay = [block_send(CROSS, RELAY, p, at_relay) for p in every]
    back = [
        send(TRANSIT, p, blocks.at[OWN, p], transit.at[p - 2], at_back) for p in (2, 3)
    ]
    across = [
        send(ACROSS, 0, blocks.at[OWN, pl.ds(0, 2)], blocks.at[ACROSS, pl.ds(0, 2)], at_across)
    ] + [send(ACROSS, p, transit.at[p - 2], blocks.at[ACROSS, p], at_back) for p in (2, 3)]
    sib = send(SIB, 0, blocks.at[OWN], blocks.at[SIB], at_sib)
    sib_cross = [block_send(CROSS, SIB2, p, at_sib) for p in every]
    sib_relay = [block_send(RELAY, SIB2, p, at_sib) for p in every]
    halo_up = send(HALO_LO, 0, edge.at[1], halo.at[0], at_up)
    halo_down = send(HALO_HI, 0, edge.at[0], halo.at[1], at_down)

    cross[0].start()
    back[0].start()
    back[1].start()
    across[0].start()
    for p in (1, 2, 3):
        cross[p].start()
    sib.start()

    for copy in loads:
        copy.wait()
    fields[...] = fields_in[...].astype(jnp.float32)

    def chosen(target):
        target = lax.rem(target + NBLK, NBLK)
        total = None
        for n in range(1, NNZ - 1):
            keep = (list_ref[0, n] == target).astype(jnp.float32)
            term = keep * couple[n].astype(jnp.float32)
            total = term if total is None else total + term
        return total

    def side_by_side(first, second):
        pair = jnp.concatenate([first, second], axis=-1)
        return pair.reshape(TERMS * MB, 2 * MB).astype(jnp.bfloat16)

    weights[:, 0:128] = side_by_side(couple[0].astype(jnp.float32), chosen(i + 1 - 2 * c))
    weights[:, 128:256] = side_by_side(
        couple[NNZ - 1].astype(jnp.float32), chosen(i + 2 - 4 * h)
    )
    weights[:, 256:384] = side_by_side(chosen(i - 2 + 4 * h), chosen(i - 1 + 2 * c))

    @pl.loop(0, 8)
    def _(n):
        rows = pl.ds(pl.multiple_of(n * 256, 256), 256)
        held_ref[rows, :] = base[rows, :].astype(jnp.float32) + half_step * held_ref[rows, :]

    def multiply(pos, first, last):
        plane = PLANES[pos]
        fresh = first == OWN

        @pl.loop(0, 4, unroll=2)
        def _(n):
            sy = n * 2
            s = n // 2
            depth = (last - first) * MB
            sides = [blocks[first:last, pos, sy + k].reshape(depth, 128) for k in (0, 1)]
            result = jnp.dot(
                weights[:, first * MB : last * MB],
                jnp.concatenate(sides, axis=1),
                preferred_element_type=jnp.float32,
            )
            for k in (0, 1):
                columns = slice(128 * k, 128 * (k + 1))
                term_d = result[0:MB, columns]
                yy = lax.rem(sy, 4) + k
                row = plane * 4 + yy
                term_r = fields[pl.ds(row, 1), :] * result[MB : 2 * MB, columns]
                for t in range(1, K):
                    term_r = term_r + fields[pl.ds(16 * t + row, 1), :] * result[
                        (1 + t) * MB : (2 + t) * MB, columns
                    ]
                if fresh:
                    mixed = mix_ref[s, 0] * blocks[OWN, pos, yy].astype(jnp.float32)
                    mixed = mixed + mix_ref[s, 1] * blocks[OWN, pos, 4 + yy].astype(jnp.float32)
                    diff[1 + plane, sy + k] = term_d
                    react[plane, sy + k] = term_r - mixed
                else:
                    total = diff[1 + plane, sy + k] + term_d
                    diff[1 + plane, sy + k] = total
                    react[plane, sy + k] += term_r
                    if pos < 2:
                        edge[pos, sy + k] = total.astype(jnp.bfloat16)

    def in_plane(plane, sy):
        s4 = (sy // 4) * 4
        center = diff[1 + plane, sy]
        lap = diff[1 + plane, s4 + (sy + 1) % 4] + diff[1 + plane, s4 + (sy + 3) % 4]
        lap = lap + (pltpu.roll(center, 1, 1) + pltpu.roll(center, 127, 1))
        return lap - 6.0 * center

    def pass_on(copies, yes, p):
        @pl.when(yes)
        def _():
            copies[p].start()

    def take_cross(p):
        cross[p].wait_recv()
        relay[p].start()
        pass_on(sib_cross, c == h, p)

    def take_relay(p):
        relay[p].wait_recv()
        pass_on(sib_relay, c != h, p)

    take_cross(0)
    take_cross(1)
    for n in (0, 1):
        back[n].wait_recv()
        across[1 + n].start()
    sib.wait_recv()
    across[0].wait_recv()
    multiply(0, OWN, RELAY)
    take_cross(2)
    take_relay(0)
    multiply(1, OWN, RELAY)
    take_cross(3)
    take_relay(1)
    for p in (0, 1):
        sib_cross[p].wait_recv()
        multiply(p, RELAY, SIB2 + 1)

    @pl.when(c == 1)
    def _():
        pl.semaphore_wait(barrier, 2)
        signal(slabs_sem, at_sib)

    @pl.when(c == 0)
    def _():
        pl.semaphore_wait(slabs_sem, 1)

    halo_up.start()
    halo_down.start()

    for plane in (0, 3):
        for sy in range(8):
            react[plane, sy] -= diffusivity_ref[sy // 4] * in_plane(plane, sy)

    for n in (0, 1):
        across[1 + n].wait_recv()
        multiply(2 + n, OWN, RELAY)
    for p in (2, 3):
        take_relay(p)
        sib_cross[p].wait_recv()
        multiply(p, RELAY, SIB2 + 1)
    halo_up.wait_recv()
    halo_down.wait_recv()

    for sy in range(8):
        scale = diffusivity_ref[sy // 4]
        d = [diff[1 + plane, sy] for plane in range(4)]
        low = halo[0, sy].astype(jnp.float32)
        high = halo[1, sy].astype(jnp.float32)
        parts = (
            low + d[1],
            d[0] + d[2] + in_plane(1, sy),
            d[1] + d[3] + in_plane(2, sy),
            d[2] + high,
        )
        for plane in range(4):
            start = (sy // 4) * 16 + plane * 4 + sy % 4
            out_ref[pl.ds(start, MB, stride=STRIDE), :] = (
                react[plane, sy] - scale * parts[plane]
            )

    for copy in (*cross, *relay, *back, *across, sib, *sib_cross, halo_up, halo_down):
        copy.wait_send()


def shards(
    section_field,
    base_field,
    prev_rate,
    block_list,
    coupling,
    diffusivity,
    reaction_fields,
    species_mix,
):
    rows, species, planes, depth, width = section_field.shape
    flat = rows * species * planes * depth
    lines = species * depth
    in_hbm = pl.BlockSpec(memory_space=pltpu.HBM)
    in_vmem = pl.BlockSpec(memory_space=pltpu.VMEM)
    minus_rate, held = pl.pallas_call(
        kernel,
        name="galerkin",
        out_shape=(
            pltpu.VMEM((flat, width), jnp.float32),
            pltpu.VMEM((flat, width), jnp.float32),
        ),
        in_specs=[in_hbm] * 8,
        out_specs=(in_vmem, in_vmem),
        scratch_shapes=[
            pltpu.SMEM(block_list.shape, block_list.dtype),
            pltpu.SMEM(diffusivity.shape, diffusivity.dtype),
            pltpu.SMEM(species_mix.shape, species_mix.dtype),
            pltpu.VMEM((flat, width), jnp.bfloat16),
            pltpu.VMEM((flat, width), jnp.bfloat16),
            pltpu.VMEM((flat, width), jnp.float32),
            pltpu.VMEM((NNZ, TERMS, MB, MB), jnp.bfloat16),
            pltpu.VMEM((K * planes * depth, width), jnp.bfloat16),
            pltpu.VMEM((K * planes * depth, width), jnp.float32),
            pltpu.VMEM((6, planes, lines, MB, width), jnp.bfloat16),
            pltpu.VMEM((2, lines, MB, width), jnp.bfloat16),
            pltpu.VMEM((TERMS * MB, 6 * MB), jnp.bfloat16),
            pltpu.VMEM((planes + 2, lines, MB, width), jnp.float32),
            pltpu.VMEM((planes, lines, MB, width), jnp.float32),
            pltpu.VMEM((2, lines, MB, width), jnp.bfloat16),
            pltpu.VMEM((2, lines, MB, width), jnp.bfloat16),
            pltpu.SemaphoreType.DMA((8,)),
            pltpu.SemaphoreType.DMA((9, 4)),
            pltpu.SemaphoreType.DMA((9, 4)),
            pltpu.SemaphoreType.REGULAR,
            pltpu.SemaphoreType.REGULAR,
        ],
        compiler_params=pltpu.CompilerParams(
            collective_id=0, has_side_effects=True, vmem_limit_bytes=57 * 1024 * 1024
        ),
        cost_estimate=pl.CostEstimate(
            flops=2 * TERMS * 6 * MB * MB * species * planes * depth * width,
            bytes_accessed=2**21,
            transcendentals=0,
        ),
    )(
        section_field.reshape(flat, width),
        coupling.reshape(NNZ, TERMS, MB, MB),
        reaction_fields.reshape(K * planes * depth, width),
        block_list,
        diffusivity,
        species_mix,
        base_field.reshape(flat, width),
        prev_rate.reshape(flat, width),
    )
    rate = -minus_rate
    next_field = (held - half_step * minus_rate).astype(jnp.bfloat16)
    return (rate.reshape(section_field.shape), next_field.reshape(section_field.shape))


def solution(mesh):
    placed = (
        P("mode", None, "gx", None, None),
        P("mode", None, "gx", None, None),
        P("mode", None, "gx", None, None),
        P("mode", None),
        P("mode", None, None, None, None),
        P(),
        P(None, "gx", None, None),
        P(),
    )
    return jax.shard_map(
        shards,
        mesh=mesh,
        in_specs=placed,
        out_specs=(P("mode", None, "gx", None, None), P("mode", None, "gx", None, None)),
        check_vma=False,
    )
```

```python
import jax
import jax.numpy as jnp
from jax import lax
from jax.sharding import PartitionSpec as P
import jax.experimental.pallas as pl
import jax.experimental.pallas.tpu as pltpu

MB = 64
NBLK = 16
K = 4
TERMS = 1 + K
NNZ = 5
MESH = pl.DeviceIdType.MESH

half_step = 0.25

OWN, SIB, ACROSS, CROSS, RELAY, SIB2 = range(6)
TRANSIT, HALO_LO, HALO_HI = 6, 7, 8
PLANES = (3, 0, 1, 2)
PIECE = 512
STRIDE = 32


def kernel(
    section_hbm,
    coupling_hbm,
    fields_hbm,
    list_hbm,
    diffusivity_hbm,
    mix_hbm,
    base_hbm,
    prev_hbm,
    out_ref,
    held_ref,
    list_ref,
    diffusivity_ref,
    mix_ref,
    base,
    native,
    wide,
    couple,
    fields_in,
    fields,
    blocks,
    transit,
    weights,
    diff,
    react,
    edge,
    halo,
    own_sem,
    local_sem,
    send_sem,
    recv_sem,
    ready_sem,
    slabs_sem,
):
    g = lax.axis_index("gx")
    i = lax.axis_index("mode")
    y = i // 4
    h = lax.rem(i // 2, 2)
    c = lax.rem(i, 2)
    step = 1 - 2 * h

    def device(dy, hh, cc):
        return (g, lax.rem(y + dy + 4, 4) * 4 + hh * 2 + cc)

    at_cross = device(0, 1 - h, c)
    at_relay = device(step, h, c)
    at_back = device(-step, h, c)
    at_across = device(2, h, c)
    at_sib = device(0, h, 1 - c)
    at_up = (lax.rem(g + 1, 16), i)
    at_down = (lax.rem(g + 15, 16), i)

    def signal(sem, peer):
        pl.semaphore_signal(sem, inc=1, device_id=peer, device_id_type=MESH)

    pieces = [pl.ds(n * PIECE, PIECE) for n in range(section_hbm.shape[0] // PIECE)]
    own = [
        pltpu.make_async_copy(section_hbm.at[rows], native.at[rows], own_sem.at[n])
        for n, rows in enumerate(pieces)
    ]
    for copy in own:
        copy.start()
    loads = [
        pltpu.make_async_copy(source, target, local_sem.at[n])
        for n, (source, target) in enumerate(
            (
                (coupling_hbm, couple),
                (fields_hbm, fields_in),
                (list_hbm, list_ref),
                (diffusivity_hbm, diffusivity_ref),
                (mix_hbm, mix_ref),
                (base_hbm, base),
                (prev_hbm, held_ref),
            )
        )
    ]

    barrier = pltpu.get_barrier_semaphore()
    for peer in (device(0, 1 - h, 0), device(1, h, 0), device(3, h, 0), device(2, h, 0)):
        signal(barrier, peer)

    @pl.when(c == 1)
    def _():
        signal(barrier, at_sib)

    for copy in loads:
        copy.start()

    for copy, rows in zip(own, pieces):
        copy.wait()
        wide[rows, :] = native[rows, :].astype(jnp.float32)

    def arrange(pos):
        for sy in range(8):
            start = (sy // 4) * 16 + PLANES[pos] * 4 + sy % 4
            blocks[OWN, pos, sy] = wide[pl.ds(start, MB, stride=STRIDE), :].astype(jnp.bfloat16)

    arrange(0)
    arrange(1)

    @pl.when(c == 0)
    def _():
        pl.semaphore_wait(barrier, 9)
        signal(ready_sem, at_sib)

    @pl.when(c == 1)
    def _():
        pl.semaphore_wait(ready_sem, 1)
        signal(barrier, at_up)
        signal(barrier, at_down)

    def send(kind, part, source, target, peer):
        return pltpu.make_async_remote_copy(
            src_ref=source,
            dst_ref=target,
            send_sem=send_sem.at[kind, part],
            recv_sem=recv_sem.at[kind, part],
            device_id=peer,
            device_id_type=MESH,
        )

    def block_send(source, target, pos, peer):
        return send(target, pos, blocks.at[source, pos], blocks.at[target, pos], peer)

    every = range(4)
    cross = [block_send(OWN, CROSS, p, at_cross) for p in every]
    relay = [block_send(CROSS, RELAY, p, at_relay) for p in every]
    back = [
        send(TRANSIT, p, blocks.at[OWN, p], transit.at[p - 2], at_back) for p in (2, 3)
    ]
    across = [block_send(OWN, ACROSS, p, at_across) for p in (0, 1)] + [
        send(ACROSS, p, transit.at[p - 2], blocks.at[ACROSS, p], at_back) for p in (2, 3)
    ]
    sib = send(SIB, 0, blocks.at[OWN], blocks.at[SIB], at_sib)
    sib_cross = [block_send(CROSS, SIB2, p, at_sib) for p in every]
    sib_relay = [block_send(RELAY, SIB2, p, at_sib) for p in every]
    halo_up = send(HALO_LO, 0, edge.at[0], halo.at[0], at_up)
    halo_down = send(HALO_HI, 0, edge.at[1], halo.at[1], at_down)

    cross[0].start()
    across[0].start()
    cross[1].start()
    across[1].start()
    arrange(2)
    cross[2].start()
    back[0].start()
    arrange(3)
    cross[3].start()
    back[1].start()
    sib.start()

    for copy in loads:
        copy.wait()
    fields[...] = fields_in[...].astype(jnp.float32)

    def chosen(target):
        target = lax.rem(target + NBLK, NBLK)
        total = None
        for n in range(1, NNZ - 1):
            keep = (list_ref[0, n] == target).astype(jnp.float32)
            term = keep * couple[n].astype(jnp.float32)
            total = term if total is None else total + term
        return total

    def side_by_side(first, second):
        pair = jnp.concatenate([first, second], axis=-1)
        return pair.reshape(TERMS * MB, 2 * MB).astype(jnp.bfloat16)

    weights[:, 0:128] = side_by_side(couple[0].astype(jnp.float32), chosen(i + 1 - 2 * c))
    weights[:, 128:256] = side_by_side(
        couple[NNZ - 1].astype(jnp.float32), chosen(i + 2 - 4 * h)
    )
    weights[:, 256:384] = side_by_side(chosen(i - 2 + 4 * h), chosen(i - 1 + 2 * c))

    @pl.loop(0, 8)
    def _(n):
        rows = pl.ds(pl.multiple_of(n * 256, 256), 256)
        held_ref[rows, :] = base[rows, :].astype(jnp.float32) + half_step * held_ref[rows, :]

    def multiply(pos, first, last):
        plane = PLANES[pos]
        fresh = first == OWN

        @pl.loop(0, 4, unroll=2)
        def _(n):
            sy = n * 2
            s = n // 2
            depth = (last - first) * MB
            sides = [blocks[first:last, pos, sy + k].reshape(depth, 128) for k in (0, 1)]
            result = jnp.dot(
                weights[:, first * MB : last * MB],
                jnp.concatenate(sides, axis=1),
                preferred_element_type=jnp.float32,
            )
            for k in (0, 1):
                columns = slice(128 * k, 128 * (k + 1))
                term_d = result[0:MB, columns]
                yy = lax.rem(sy, 4) + k
                row = plane * 4 + yy
                term_r = fields[pl.ds(row, 1), :] * result[MB : 2 * MB, columns]
                for t in range(1, K):
                    term_r = term_r + fields[pl.ds(16 * t + row, 1), :] * result[
                        (1 + t) * MB : (2 + t) * MB, columns
                    ]
                if fresh:
                    mixed = mix_ref[s, 0] * blocks[OWN, pos, yy].astype(jnp.float32)
                    mixed = mixed + mix_ref[s, 1] * blocks[OWN, pos, 4 + yy].astype(jnp.float32)
                    diff[1 + plane, sy + k] = term_d
                    react[plane, sy + k] = term_r - mixed
                else:
                    total = diff[1 + plane, sy + k] + term_d
                    diff[1 + plane, sy + k] = total
                    react[plane, sy + k] += term_r
                    if pos < 2:
                        edge[pos, sy + k] = total.astype(jnp.bfloat16)

    def in_plane(plane, sy):
        s4 = (sy // 4) * 4
        center = diff[1 + plane, sy]
        lap = diff[1 + plane, s4 + (sy + 1) % 4] + diff[1 + plane, s4 + (sy + 3) % 4]
        lap = lap + (pltpu.roll(center, 1, 1) + pltpu.roll(center, 127, 1))
        return lap - 6.0 * center

    def pass_on(copies, yes, p):
        @pl.when(yes)
        def _():
            copies[p].start()

    def take_cross(p):
        cross[p].wait_recv()
        relay[p].start()
        pass_on(sib_cross, c == h, p)

    def take_relay(p):
        relay[p].wait_recv()
        pass_on(sib_relay, c != h, p)

    def slab_entered():
        @pl.when(c == 1)
        def _():
            pl.semaphore_wait(barrier, 2)
            signal(slabs_sem, at_sib)

        @pl.when(c == 0)
        def _():
            pl.semaphore_wait(slabs_sem, 1)

    def late(pos):
        take_relay(pos)
        sib_cross[pos].wait_recv()
        multiply(pos, RELAY, SIB2 + 1)

    def lessen(plane, others):
        for sy in range(8):
            part = in_plane(plane, sy)
            for other in others:
                part = part + diff[1 + other, sy]
            react[plane, sy] -= diffusivity_ref[sy // 4] * part

    def finish(plane, sy, part):
        start = (sy // 4) * 16 + plane * 4 + sy % 4
        out_ref[pl.ds(start, MB, stride=STRIDE), :] = (
            react[plane, sy] - diffusivity_ref[sy // 4] * part
        )

    take_cross(0)
    sib.wait_recv()
    across[0].wait_recv()
    multiply(0, OWN, RELAY)
    take_cross(1)
    back[0].wait_recv()
    across[2].start()
    late(0)
    slab_entered()
    halo_up.start()
    across[1].wait_recv()
    take_cross(2)
    multiply(1, OWN, RELAY)
    back[1].wait_recv()
    across[3].start()
    late(1)
    halo_down.start()
    take_cross(3)
    across[2].wait_recv()
    multiply(2, OWN, RELAY)
    lessen(3, ())
    lessen(0, ())
    late(2)
    lessen(1, (0,))
    across[3].wait_recv()
    multiply(3, OWN, RELAY)
    late(3)
    for sy in range(8):
        inner = diff[3, sy]
        finish(1, sy, inner)
        finish(2, sy, in_plane(2, sy) + (diff[2, sy] + diff[4, sy]))
    halo_down.wait_recv()
    for sy in range(8):
        finish(3, sy, diff[3, sy] + halo[1, sy].astype(jnp.float32))
    halo_up.wait_recv()
    for sy in range(8):
        finish(0, sy, diff[2, sy] + halo[0, sy].astype(jnp.float32))

    for copy in (*cross, *relay, *back, *across, sib, *sib_cross, halo_up, halo_down):
        copy.wait_send()


def shards(
    section_field,
    base_field,
    prev_rate,
    block_list,
    coupling,
    diffusivity,
    reaction_fields,
    species_mix,
):
    rows, species, planes, depth, width = section_field.shape
    flat = rows * species * planes * depth
    lines = species * depth
    in_hbm = pl.BlockSpec(memory_space=pltpu.HBM)
    in_vmem = pl.BlockSpec(memory_space=pltpu.VMEM)
    minus_rate, held = pl.pallas_call(
        kernel,
        name="galerkin",
        out_shape=(
            pltpu.VMEM((flat, width), jnp.float32),
            pltpu.VMEM((flat, width), jnp.float32),
        ),
        in_specs=[in_hbm] * 8,
        out_specs=(in_vmem, in_vmem),
        scratch_shapes=[
            pltpu.SMEM(block_list.shape, block_list.dtype),
            pltpu.SMEM(diffusivity.shape, diffusivity.dtype),
            pltpu.SMEM(species_mix.shape, species_mix.dtype),
            pltpu.VMEM((flat, width), jnp.bfloat16),
            pltpu.VMEM((flat, width), jnp.bfloat16),
            pltpu.VMEM((flat, width), jnp.float32),
            pltpu.VMEM((NNZ, TERMS, MB, MB), jnp.bfloat16),
            pltpu.VMEM((K * planes * depth, width), jnp.bfloat16),
            pltpu.VMEM((K * planes * depth, width), jnp.float32),
            pltpu.VMEM((6, planes, lines, MB, width), jnp.bfloat16),
            pltpu.VMEM((2, lines, MB, width), jnp.bfloat16),
            pltpu.VMEM((TERMS * MB, 6 * MB), jnp.bfloat16),
            pltpu.VMEM((planes + 2, lines, MB, width), jnp.float32),
            pltpu.VMEM((planes, lines, MB, width), jnp.float32),
            pltpu.VMEM((2, lines, MB, width), jnp.bfloat16),
            pltpu.VMEM((2, lines, MB, width), jnp.bfloat16),
            pltpu.SemaphoreType.DMA((flat // PIECE,)),
            pltpu.SemaphoreType.DMA((7,)),
            pltpu.SemaphoreType.DMA((9, 4)),
            pltpu.SemaphoreType.DMA((9, 4)),
            pltpu.SemaphoreType.REGULAR,
            pltpu.SemaphoreType.REGULAR,
        ],
        compiler_params=pltpu.CompilerParams(
            collective_id=0, has_side_effects=True, vmem_limit_bytes=57 * 1024 * 1024
        ),
        cost_estimate=pl.CostEstimate(
            flops=2 * TERMS * 6 * MB * MB * species * planes * depth * width,
            bytes_accessed=2**21,
            transcendentals=0,
        ),
    )(
        section_field.reshape(flat, width),
        coupling.reshape(NNZ, TERMS, MB, MB),
        reaction_fields.reshape(K * planes * depth, width),
        block_list,
        diffusivity,
        species_mix,
        base_field.reshape(flat, width),
        prev_rate.reshape(flat, width),
    )
    rate = -minus_rate
    next_field = (held - half_step * minus_rate).astype(jnp.bfloat16)
    return (rate.reshape(section_field.shape), next_field.reshape(section_field.shape))


def solution(mesh):
    placed = (
        P("mode", None, "gx", None, None),
        P("mode", None, "gx", None, None),
        P("mode", None, "gx", None, None),
        P("mode", None),
        P("mode", None, None, None, None),
        P(),
        P(None, "gx", None, None),
        P(),
    )
    return jax.shard_map(
        shards,
        mesh=mesh,
        in_specs=placed,
        out_specs=(P("mode", None, "gx", None, None), P("mode", None, "gx", None, None)),
        check_vma=False,
    )
```

```python
import jax
import jax.numpy as jnp
from jax import lax
from jax.sharding import PartitionSpec as P
import jax.experimental.pallas as pl
import jax.experimental.pallas.tpu as pltpu

MB = 64
NBLK = 16
K = 4
TERMS = 1 + K
NNZ = 5
MESH = pl.DeviceIdType.MESH

half_step = 0.25

OWN, SIB, ACROSS, CROSS, RELAY, SIB2 = range(6)
TRANSIT, HALO_LO, HALO_HI = 6, 7, 8
PLANES = (3, 0, 1, 2)
PIECE = 512
STRIDE = 32


def kernel(
    section_hbm,
    coupling_hbm,
    fields_hbm,
    list_hbm,
    diffusivity_hbm,
    mix_hbm,
    base_hbm,
    prev_hbm,
    out_ref,
    held_ref,
    list_ref,
    diffusivity_ref,
    mix_ref,
    base,
    native,
    wide,
    couple,
    fields_in,
    fields,
    blocks,
    transit,
    weights,
    diff,
    react,
    edge,
    halo,
    own_sem,
    local_sem,
    send_sem,
    recv_sem,
    ready_sem,
    gather_sem,
    slabs_sem,
):
    g = lax.axis_index("gx")
    i = lax.axis_index("mode")
    y = i // 4
    h = lax.rem(i // 2, 2)
    c = lax.rem(i, 2)
    step = 1 - 2 * h

    def device(dy, hh, cc):
        return (g, lax.rem(y + dy + 4, 4) * 4 + hh * 2 + cc)

    at_cross = device(0, 1 - h, c)
    at_relay = device(step, h, c)
    at_back = device(-step, h, c)
    at_across = device(2, h, c)
    at_sib = device(0, h, 1 - c)
    at_up = (lax.rem(g + 1, 16), i)
    at_down = (lax.rem(g + 15, 16), i)

    def signal(sem, peer):
        pl.semaphore_signal(sem, inc=1, device_id=peer, device_id_type=MESH)

    pieces = [pl.ds(n * PIECE, PIECE) for n in range(section_hbm.shape[0] // PIECE)]
    own = [
        pltpu.make_async_copy(section_hbm.at[rows], native.at[rows], own_sem.at[n])
        for n, rows in enumerate(pieces)
    ]
    for copy in own:
        copy.start()
    loads = [
        pltpu.make_async_copy(source, target, local_sem.at[n])
        for n, (source, target) in enumerate(
            (
                (coupling_hbm, couple),
                (fields_hbm, fields_in),
                (list_hbm, list_ref),
                (diffusivity_hbm, diffusivity_ref),
                (mix_hbm, mix_ref),
                (base_hbm, base),
                (prev_hbm, held_ref),
            )
        )
    ]

    first = y == 0
    second = y == 1
    barrier = pltpu.get_barrier_semaphore()

    @pl.when(jnp.logical_not(first))
    def _():
        signal(barrier, at_cross)
        signal(barrier, at_sib)

    for dy in (1, 2, 3):

        @pl.when(lax.rem(y + dy, 4) != 0)
        def _(dy=dy):
            signal(barrier, device(dy, h, c))

    @pl.when(first)
    def _():
        signal(barrier, device(1, 1 - h, c))
        signal(barrier, device(1, h, 1 - c))

    for copy in loads:
        copy.start()

    for copy, rows in zip(own, pieces):
        copy.wait()
        wide[rows, :] = native[rows, :].astype(jnp.float32)

    def arrange(pos):
        for sy in range(8):
            start = (sy // 4) * 16 + PLANES[pos] * 4 + sy % 4
            blocks[OWN, pos, sy] = wide[pl.ds(start, MB, stride=STRIDE), :].astype(jnp.bfloat16)

    arrange(0)
    arrange(1)

    @pl.when(second)
    def _():
        pl.semaphore_wait(barrier, 7)
        signal(ready_sem, device(3, h, c))

    @pl.when(y > 1)
    def _():
        pl.semaphore_wait(barrier, 5)
        signal(gather_sem, device(4 - y, h, c))

    @pl.when(first)
    def _():
        pl.semaphore_wait(ready_sem, 1)

    def send(kind, part, source, target, peer):
        return pltpu.make_async_remote_copy(
            src_ref=source,
            dst_ref=target,
            send_sem=send_sem.at[kind, part],
            recv_sem=recv_sem.at[kind, part],
            device_id=peer,
            device_id_type=MESH,
        )

    def block_send(source, target, pos, peer):
        return send(target, pos, blocks.at[source, pos], blocks.at[target, pos], peer)

    every = range(4)
    cross = [block_send(OWN, CROSS, p, at_cross) for p in every]
    relay = [block_send(CROSS, RELAY, p, at_relay) for p in every]
    back = [
        send(TRANSIT, p, blocks.at[OWN, p], transit.at[p - 2], at_back) for p in (2, 3)
    ]
    across = [block_send(OWN, ACROSS, p, at_across) for p in (0, 1)] + [
        send(ACROSS, p, transit.at[p - 2], blocks.at[ACROSS, p], at_back) for p in (2, 3)
    ]
    sib = send(SIB, 0, blocks.at[OWN], blocks.at[SIB], at_sib)
    sib_cross = [block_send(CROSS, SIB2, p, at_sib) for p in every]
    sib_relay = [block_send(RELAY, SIB2, p, at_sib) for p in every]
    halo_up = send(HALO_LO, 0, edge.at[0], halo.at[0], at_up)
    halo_down = send(HALO_HI, 0, edge.at[1], halo.at[1], at_down)

    cross[0].start()
    across[0].start()
    arrange(2)
    back[0].start()
    cross[1].start()
    across[1].start()
    arrange(3)
    back[1].start()
    cross[2].start()
    cross[3].start()
    sib.start()

    @pl.when(first)
    def _():
        pl.semaphore_wait(gather_sem, 2)
        signal(barrier, at_up)
        signal(barrier, at_down)

    for copy in loads:
        copy.wait()
    fields[...] = fields_in[...].astype(jnp.float32)

    def chosen(target):
        target = lax.rem(target + NBLK, NBLK)
        total = None
        for n in range(1, NNZ - 1):
            keep = (list_ref[0, n] == target).astype(jnp.float32)
            term = keep * couple[n].astype(jnp.float32)
            total = term if total is None else total + term
        return total

    def side_by_side(first, second):
        pair = jnp.concatenate([first, second], axis=-1)
        return pair.reshape(TERMS * MB, 2 * MB).astype(jnp.bfloat16)

    weights[:, 0:128] = side_by_side(couple[0].astype(jnp.float32), chosen(i + 1 - 2 * c))
    weights[:, 128:256] = side_by_side(
        couple[NNZ - 1].astype(jnp.float32), chosen(i + 2 - 4 * h)
    )
    weights[:, 256:384] = side_by_side(chosen(i - 2 + 4 * h), chosen(i - 1 + 2 * c))

    @pl.loop(0, 8)
    def _(n):
        rows = pl.ds(n * 8, 8)
        held_ref[rows] = base[rows].astype(jnp.float32) + half_step * held_ref[rows]

    def multiply(pos, first, last):
        plane = PLANES[pos]
        fresh = first == OWN

        @pl.loop(0, 4, unroll=4)
        def _(n):
            sy = n * 2
            s = n // 2
            depth = (last - first) * MB
            sides = [blocks[first:last, pos, sy + k].reshape(depth, 128) for k in (0, 1)]
            result = jnp.dot(
                weights[:, first * MB : last * MB],
                jnp.concatenate(sides, axis=1),
                preferred_element_type=jnp.float32,
            )
            for k in (0, 1):
                columns = slice(128 * k, 128 * (k + 1))
                term_d = result[0:MB, columns]
                yy = lax.rem(sy, 4) + k
                row = plane * 4 + yy
                term_r = fields[pl.ds(row, 1), :] * result[MB : 2 * MB, columns]
                for t in range(1, K):
                    term_r = term_r + fields[pl.ds(16 * t + row, 1), :] * result[
                        (1 + t) * MB : (2 + t) * MB, columns
                    ]
                if fresh:
                    mixed = mix_ref[s, 0] * blocks[OWN, pos, yy].astype(jnp.float32)
                    mixed = mixed + mix_ref[s, 1] * blocks[OWN, pos, 4 + yy].astype(jnp.float32)
                    diff[1 + plane, sy + k] = term_d
                    react[plane, sy + k] = term_r - mixed
                else:
                    total = diff[1 + plane, sy + k] + term_d
                    diff[1 + plane, sy + k] = total
                    react[plane, sy + k] += term_r
                    if pos < 2:
                        edge[pos, sy + k] = total.astype(jnp.bfloat16)

    def in_plane(plane, sy):
        s4 = (sy // 4) * 4
        center = diff[1 + plane, sy]
        lap = diff[1 + plane, s4 + (sy + 1) % 4] + diff[1 + plane, s4 + (sy + 3) % 4]
        lap = lap + (pltpu.roll(center, 1, 1) + pltpu.roll(center, 127, 1))
        return lap - 6.0 * center

    def pass_on(copies, yes, p):
        @pl.when(yes)
        def _():
            copies[p].start()

    def take_cross(p):
        cross[p].wait_recv()
        relay[p].start()
        pass_on(sib_cross, c == h, p)

    def take_relay(p):
        relay[p].wait_recv()
        pass_on(sib_relay, c != h, p)

    def late(pos):
        sib_cross[pos].wait_recv()
        multiply(pos, RELAY, SIB2 + 1)

    def lessen(plane, others):
        for sy in range(8):
            part = in_plane(plane, sy)
            for other in others:
                part = part + diff[1 + other, sy]
            react[plane, sy] -= diffusivity_ref[sy // 4] * part

    def finish():
        @pl.loop(0, MB // 16, unroll=4)
        def _(n):
            rows = pl.ds(pl.multiple_of(16 * n, 16), 16)

            def at(plane, sy):
                return diff[1 + plane, sy, rows, :]

            def in_plane_rows(plane, sy):
                s4 = (sy // 4) * 4
                center = at(plane, sy)
                lap = at(plane, s4 + (sy + 1) % 4) + at(plane, s4 + (sy + 3) % 4)
                lap = lap + (pltpu.roll(center, 1, 1) + pltpu.roll(center, 127, 1))
                return lap - 6.0 * center

            for s in range(2):
                for pair in range(2):
                    lines = []
                    for plane in (2 * pair, 2 * pair + 1):
                        for sy in range(4 * s, 4 * s + 4):
                            if plane == 0:
                                part = at(1, sy) + halo[0, sy, rows, :].astype(jnp.float32)
                            elif plane == 1:
                                part = at(2, sy)
                            elif plane == 2:
                                part = in_plane_rows(2, sy) + (at(1, sy) + at(3, sy))
                            else:
                                part = at(2, sy) + halo[1, sy, rows, :].astype(jnp.float32)
                            lines.append(
                                react[plane, sy, rows, :] - diffusivity_ref[s] * part
                            )
                    out_ref[rows, pl.ds(8 * (2 * s + pair), 8), :] = jnp.swapaxes(
                        jnp.stack(lines, axis=0), 0, 1
                    )

    take_cross(0)
    take_cross(1)
    back[0].wait_recv()
    across[2].start()
    sib.wait_recv()
    across[0].wait_recv()
    multiply(0, OWN, RELAY)
    take_relay(0)

    @pl.when(first)
    def _():
        pl.semaphore_wait(barrier, 2)
        for dy in (1, 2, 3):
            signal(slabs_sem, device(dy, h, c))

    late(0)

    @pl.when(jnp.logical_not(first))
    def _():
        pl.semaphore_wait(slabs_sem, 1)

    halo_up.start()
    take_cross(2)
    across[1].wait_recv()
    multiply(1, OWN, RELAY)
    back[1].wait_recv()
    across[3].start()
    take_cross(3)
    take_relay(1)
    lessen(3, ())
    late(1)
    halo_down.start()
    lessen(0, ())
    across[2].wait_recv()
    multiply(2, OWN, RELAY)
    take_relay(2)
    late(2)
    lessen(1, (0,))
    across[3].wait_recv()
    multiply(3, OWN, RELAY)
    take_relay(3)
    late(3)
    halo_down.wait_recv()
    halo_up.wait_recv()
    finish()

    for copy in (*cross, *relay, *back, *across, sib, *sib_cross, halo_up, halo_down):
        copy.wait_send()


def shards(
    section_field,
    base_field,
    prev_rate,
    block_list,
    coupling,
    diffusivity,
    reaction_fields,
    species_mix,
):
    rows, species, planes, depth, width = section_field.shape
    flat = rows * species * planes * depth
    lines = species * depth
    in_hbm = pl.BlockSpec(memory_space=pltpu.HBM)
    in_vmem = pl.BlockSpec(memory_space=pltpu.VMEM)
    minus_rate, held = pl.pallas_call(
        kernel,
        name="galerkin",
        out_shape=(
            pltpu.VMEM((rows, STRIDE, width), jnp.float32),
            pltpu.VMEM((rows, STRIDE, width), jnp.float32),
        ),
        in_specs=[in_hbm] * 8,
        out_specs=(in_vmem, in_vmem),
        scratch_shapes=[
            pltpu.SMEM(block_list.shape, block_list.dtype),
            pltpu.SMEM(diffusivity.shape, diffusivity.dtype),
            pltpu.SMEM(species_mix.shape, species_mix.dtype),
            pltpu.VMEM((rows, STRIDE, width), jnp.bfloat16),
            pltpu.VMEM((flat, width), jnp.bfloat16),
            pltpu.VMEM((flat, width), jnp.float32),
            pltpu.VMEM((NNZ, TERMS, MB, MB), jnp.bfloat16),
            pltpu.VMEM((K * planes * depth, width), jnp.bfloat16),
            pltpu.VMEM((K * planes * depth, width), jnp.float32),
            pltpu.VMEM((6, planes, lines, MB, width), jnp.bfloat16),
            pltpu.VMEM((2, lines, MB, width), jnp.bfloat16),
            pltpu.VMEM((TERMS * MB, 6 * MB), jnp.bfloat16),
            pltpu.VMEM((planes + 2, lines, MB, width), jnp.float32),
            pltpu.VMEM((planes, lines, MB, width), jnp.float32),
            pltpu.VMEM((2, lines, MB, width), jnp.bfloat16),
            pltpu.VMEM((2, lines, MB, width), jnp.bfloat16),
            pltpu.SemaphoreType.DMA((flat // PIECE,)),
            pltpu.SemaphoreType.DMA((7,)),
            pltpu.SemaphoreType.DMA((9, 4)),
            pltpu.SemaphoreType.DMA((9, 4)),
            pltpu.SemaphoreType.REGULAR,
            pltpu.SemaphoreType.REGULAR,
            pltpu.SemaphoreType.REGULAR,
        ],
        compiler_params=pltpu.CompilerParams(
            collective_id=0, has_side_effects=True, vmem_limit_bytes=57 * 1024 * 1024
        ),
        cost_estimate=pl.CostEstimate(
            flops=2 * TERMS * 6 * MB * MB * species * planes * depth * width,
            bytes_accessed=2**21,
            transcendentals=0,
        ),
    )(
        section_field.reshape(flat, width),
        coupling.reshape(NNZ, TERMS, MB, MB),
        reaction_fields.reshape(K * planes * depth, width),
        block_list,
        diffusivity,
        species_mix,
        base_field.reshape(rows, STRIDE, width),
        prev_rate.reshape(rows, STRIDE, width),
    )
    rate = -minus_rate
    next_field = (held - half_step * minus_rate).astype(jnp.bfloat16)
    return (rate.reshape(section_field.shape), next_field.reshape(section_field.shape))


def solution(mesh):
    placed = (
        P("mode", None, "gx", None, None),
        P("mode", None, "gx", None, None),
        P("mode", None, "gx", None, None),
        P("mode", None),
        P("mode", None, None, None, None),
        P(),
        P(None, "gx", None, None),
        P(),
    )
    return jax.shard_map(
        shards,
        mesh=mesh,
        in_specs=placed,
        out_specs=(P("mode", None, "gx", None, None), P("mode", None, "gx", None, None)),
        check_vma=False,
    )
```

```python
import jax
import jax.numpy as jnp
from jax import lax
from jax.sharding import PartitionSpec as P
import jax.experimental.pallas as pl
import jax.experimental.pallas.tpu as pltpu

MB = 64
NBLK = 16
K = 4
TERMS = 1 + K
NNZ = 5
MESH = pl.DeviceIdType.MESH

half_step = 0.25

OWN, SIB, ACROSS, CROSS, RELAY, SIB2 = range(6)
TRANSIT, HALO_LO, HALO_HI = 6, 7, 8
PLANES = (3, 0, 1, 2)
PIECE = 512
STRIDE = 32


def kernel(
    section_hbm,
    coupling_hbm,
    fields_hbm,
    list_hbm,
    diffusivity_hbm,
    mix_hbm,
    base_hbm,
    prev_hbm,
    out_ref,
    held_ref,
    list_ref,
    diffusivity_ref,
    mix_ref,
    base,
    native,
    wide,
    couple,
    fields_in,
    fields,
    blocks,
    transit,
    weights,
    diff,
    react,
    edge,
    halo,
    own_sem,
    local_sem,
    send_sem,
    recv_sem,
    ready_sem,
    gather_sem,
    slabs_sem,
):
    g = lax.axis_index("gx")
    i = lax.axis_index("mode")
    y = i // 4
    h = lax.rem(i // 2, 2)
    c = lax.rem(i, 2)
    step = 1 - 2 * h

    def device(dy, hh, cc):
        return (g, lax.rem(y + dy + 4, 4) * 4 + hh * 2 + cc)

    at_cross = device(0, 1 - h, c)
    at_relay = device(step, h, c)
    at_back = device(-step, h, c)
    at_across = device(2, h, c)
    at_sib = device(0, h, 1 - c)
    flip = 1 - lax.rem(g, 2)
    at_up = (lax.rem(g + 17 - 2 * flip, 16), i)
    at_down = (lax.rem(g + 15 + 2 * flip, 16), i)

    def plane_of(plane):
        return plane + flip * (3 - 2 * plane)

    def signal(sem, peer):
        pl.semaphore_signal(sem, inc=1, device_id=peer, device_id_type=MESH)

    pieces = [pl.ds(n * PIECE, PIECE) for n in range(section_hbm.shape[0] // PIECE)]
    own = [
        pltpu.make_async_copy(section_hbm.at[rows], native.at[rows], own_sem.at[n])
        for n, rows in enumerate(pieces)
    ]
    for copy in own:
        copy.start()
    loads = [
        pltpu.make_async_copy(source, target, local_sem.at[n])
        for n, (source, target) in enumerate(
            (
                (coupling_hbm, couple),
                (fields_hbm, fields_in),
                (list_hbm, list_ref),
                (diffusivity_hbm, diffusivity_ref),
                (mix_hbm, mix_ref),
                (base_hbm, base),
                (prev_hbm, held_ref),
            )
        )
    ]

    first = y == 0
    second = y == 1
    barrier = pltpu.get_barrier_semaphore()

    @pl.when(jnp.logical_not(first))
    def _():
        signal(barrier, at_cross)
        signal(barrier, at_sib)

    for dy in (1, 2, 3):

        @pl.when(lax.rem(y + dy, 4) != 0)
        def _(dy=dy):
            signal(barrier, device(dy, h, c))

    @pl.when(first)
    def _():
        signal(barrier, device(1, 1 - h, c))
        signal(barrier, device(1, h, 1 - c))

    for copy in loads:
        copy.start()

    for copy, rows in zip(own, pieces):
        copy.wait()
        wide[rows, :] = native[rows, :].astype(jnp.float32)

    def arrange(pos):
        for sy in range(8):
            start = (sy // 4) * 16 + plane_of(PLANES[pos]) * 4 + sy % 4
            blocks[OWN, pos, sy] = wide[pl.ds(start, MB, stride=STRIDE), :].astype(jnp.bfloat16)

    arrange(0)
    arrange(1)

    @pl.when(second)
    def _():
        pl.semaphore_wait(barrier, 7)
        signal(ready_sem, device(3, h, c))

    @pl.when(y > 1)
    def _():
        pl.semaphore_wait(barrier, 5)
        signal(gather_sem, device(4 - y, h, c))

    @pl.when(first)
    def _():
        pl.semaphore_wait(ready_sem, 1)

    def send(kind, part, source, target, peer):
        return pltpu.make_async_remote_copy(
            src_ref=source,
            dst_ref=target,
            send_sem=send_sem.at[kind, part],
            recv_sem=recv_sem.at[kind, part],
            device_id=peer,
            device_id_type=MESH,
        )

    def block_send(source, target, pos, peer):
        return send(target, pos, blocks.at[source, pos], blocks.at[target, pos], peer)

    every = range(4)
    cross = [block_send(OWN, CROSS, p, at_cross) for p in every]
    relay = [block_send(CROSS, RELAY, p, at_relay) for p in every]
    back = [
        send(TRANSIT, p, blocks.at[OWN, p], transit.at[p - 2], at_back) for p in (2, 3)
    ]
    across = [block_send(OWN, ACROSS, p, at_across) for p in (0, 1)] + [
        send(ACROSS, p, transit.at[p - 2], blocks.at[ACROSS, p], at_back) for p in (2, 3)
    ]
    sib = send(SIB, 0, blocks.at[OWN], blocks.at[SIB], at_sib)
    sib_cross = [block_send(CROSS, SIB2, p, at_sib) for p in every]
    sib_relay = [block_send(RELAY, SIB2, p, at_sib) for p in every]
    halo_up = send(HALO_HI, 0, edge.at[0], halo.at[1], at_up)
    halo_down = send(HALO_LO, 0, edge.at[1], halo.at[0], at_down)

    cross[0].start()
    across[0].start()
    cross[1].start()
    across[1].start()
    arrange(2)
    back[0].start()
    arrange(3)
    back[1].start()
    cross[2].start()
    cross[3].start()
    sib.start()

    @pl.when(first)
    def _():
        pl.semaphore_wait(gather_sem, 2)
        signal(barrier, at_up)
        signal(barrier, at_down)

    for copy in loads:
        copy.wait()
    fields[...] = fields_in[...].astype(jnp.float32)

    def chosen(target):
        target = lax.rem(target + NBLK, NBLK)
        total = None
        for n in range(1, NNZ - 1):
            keep = (list_ref[0, n] == target).astype(jnp.float32)
            term = keep * couple[n].astype(jnp.float32)
            total = term if total is None else total + term
        return total

    def side_by_side(first, second):
        pair = jnp.concatenate([first, second], axis=-1)
        return pair.reshape(TERMS * MB, 2 * MB).astype(jnp.bfloat16)

    weights[:, 0:128] = side_by_side(couple[0].astype(jnp.float32), chosen(i + 1 - 2 * c))
    weights[:, 128:256] = side_by_side(
        couple[NNZ - 1].astype(jnp.float32), chosen(i + 2 - 4 * h)
    )
    weights[:, 256:384] = side_by_side(chosen(i - 2 + 4 * h), chosen(i - 1 + 2 * c))

    @pl.loop(0, 8)
    def _(n):
        rows = pl.ds(n * 8, 8)
        held_ref[rows] = base[rows].astype(jnp.float32) + half_step * held_ref[rows]

    def multiply(pos, first, last):
        plane = PLANES[pos]
        fresh = first == OWN

        @pl.loop(0, 4, unroll=4)
        def _(n):
            sy = n * 2
            s = n // 2
            depth = (last - first) * MB
            sides = [blocks[first:last, pos, sy + k].reshape(depth, 128) for k in (0, 1)]
            result = jnp.dot(
                weights[:, first * MB : last * MB],
                jnp.concatenate(sides, axis=1),
                preferred_element_type=jnp.float32,
            )
            for k in (0, 1):
                columns = slice(128 * k, 128 * (k + 1))
                term_d = result[0:MB, columns]
                yy = lax.rem(sy, 4) + k
                row = plane_of(plane) * 4 + yy
                term_r = fields[pl.ds(row, 1), :] * result[MB : 2 * MB, columns]
                for t in range(1, K):
                    term_r = term_r + fields[pl.ds(16 * t + row, 1), :] * result[
                        (1 + t) * MB : (2 + t) * MB, columns
                    ]
                if fresh:
                    mixed = mix_ref[s, 0] * blocks[OWN, pos, yy].astype(jnp.float32)
                    mixed = mixed + mix_ref[s, 1] * blocks[OWN, pos, 4 + yy].astype(jnp.float32)
                    diff[1 + plane, sy + k] = term_d
                    react[plane, sy + k] = term_r - mixed
                else:
                    total = diff[1 + plane, sy + k] + term_d
                    diff[1 + plane, sy + k] = total
                    react[plane, sy + k] += term_r
                    if pos < 2:
                        edge[pos, sy + k] = total.astype(jnp.bfloat16)

    def in_plane(plane, sy):
        s4 = (sy // 4) * 4
        center = diff[1 + plane, sy]
        lap = diff[1 + plane, s4 + (sy + 1) % 4] + diff[1 + plane, s4 + (sy + 3) % 4]
        lap = lap + (pltpu.roll(center, 1, 1) + pltpu.roll(center, 127, 1))
        return lap - 6.0 * center

    def pass_on(copies, yes, p):
        @pl.when(yes)
        def _():
            copies[p].start()

    def take_cross(p):
        cross[p].wait_recv()
        relay[p].start()
        pass_on(sib_cross, c == h, p)

    def take_relay(p):
        relay[p].wait_recv()
        pass_on(sib_relay, c != h, p)

    def late(pos):
        sib_cross[pos].wait_recv()
        multiply(pos, RELAY, SIB2 + 1)

    def lessen(plane, others):
        for sy in range(8):
            part = in_plane(plane, sy)
            for other in others:
                part = part + diff[1 + other, sy]
            react[plane, sy] -= diffusivity_ref[sy // 4] * part

    def finish(pair):
        for flipped in (0, 1):
            planes = (2 * pair + 1, 2 * pair) if flipped else (2 * pair, 2 * pair + 1)

            @pl.when(flip == flipped)
            def _(planes=planes, block=1 - pair if flipped else pair):
                finish_block(planes, block)

    def finish_block(planes, block):
        @pl.loop(0, MB // 16, unroll=4)
        def _(n):
            rows = pl.ds(pl.multiple_of(16 * n, 16), 16)

            def at(plane, sy):
                return diff[1 + plane, sy, rows, :]

            def in_plane_rows(plane, sy):
                s4 = (sy // 4) * 4
                center = at(plane, sy)
                lap = at(plane, s4 + (sy + 1) % 4) + at(plane, s4 + (sy + 3) % 4)
                lap = lap + (pltpu.roll(center, 1, 1) + pltpu.roll(center, 127, 1))
                return lap - 6.0 * center

            for s in range(2):
                lines = []
                for plane in planes:
                    for sy in range(4 * s, 4 * s + 4):
                        if plane == 0:
                            part = at(1, sy) + halo[0, sy, rows, :].astype(jnp.float32)
                        elif plane == 1:
                            part = at(2, sy)
                        elif plane == 2:
                            part = in_plane_rows(2, sy) + (at(1, sy) + at(3, sy))
                        else:
                            part = at(2, sy) + halo[1, sy, rows, :].astype(jnp.float32)
                        lines.append(react[plane, sy, rows, :] - diffusivity_ref[s] * part)
                out_ref[rows, pl.ds(8 * (2 * s + block), 8), :] = jnp.swapaxes(
                    jnp.stack(lines, axis=0), 0, 1
                )

    take_cross(0)
    take_cross(1)
    back[0].wait_recv()
    across[2].start()
    sib.wait_recv()
    across[0].wait_recv()
    multiply(0, OWN, RELAY)
    take_relay(0)

    @pl.when(first)
    def _():
        pl.semaphore_wait(barrier, 2)
        for dy in (1, 2, 3):
            signal(slabs_sem, device(dy, h, c))

    late(0)

    @pl.when(jnp.logical_not(first))
    def _():
        pl.semaphore_wait(slabs_sem, 1)

    halo_up.start()
    take_cross(2)
    across[1].wait_recv()
    multiply(1, OWN, RELAY)
    back[1].wait_recv()
    across[3].start()
    take_cross(3)
    take_relay(1)
    lessen(3, ())
    late(1)
    halo_down.start()
    lessen(0, ())
    across[2].wait_recv()
    multiply(2, OWN, RELAY)
    take_relay(2)
    late(2)
    lessen(1, (0,))
    across[3].wait_recv()
    multiply(3, OWN, RELAY)
    take_relay(3)
    late(3)
    halo_down.wait_recv()
    finish(0)
    halo_up.wait_recv()
    finish(1)

    for copy in (*cross, *relay, *back, *across, sib, *sib_cross, halo_up, halo_down):
        copy.wait_send()


def shards(
    section_field,
    base_field,
    prev_rate,
    block_list,
    coupling,
    diffusivity,
    reaction_fields,
    species_mix,
):
    rows, species, planes, depth, width = section_field.shape
    flat = rows * species * planes * depth
    lines = species * depth
    in_hbm = pl.BlockSpec(memory_space=pltpu.HBM)
    in_vmem = pl.BlockSpec(memory_space=pltpu.VMEM)
    minus_rate, held = pl.pallas_call(
        kernel,
        name="galerkin",
        out_shape=(
            pltpu.VMEM((rows, STRIDE, width), jnp.float32),
            pltpu.VMEM((rows, STRIDE, width), jnp.float32),
        ),
        in_specs=[in_hbm] * 8,
        out_specs=(in_vmem, in_vmem),
        scratch_shapes=[
            pltpu.SMEM(block_list.shape, block_list.dtype),
            pltpu.SMEM(diffusivity.shape, diffusivity.dtype),
            pltpu.SMEM(species_mix.shape, species_mix.dtype),
            pltpu.VMEM((rows, STRIDE, width), jnp.bfloat16),
            pltpu.VMEM((flat, width), jnp.bfloat16),
            pltpu.VMEM((flat, width), jnp.float32),
            pltpu.VMEM((NNZ, TERMS, MB, MB), jnp.bfloat16),
            pltpu.VMEM((K * planes * depth, width), jnp.bfloat16),
            pltpu.VMEM((K * planes * depth, width), jnp.float32),
            pltpu.VMEM((6, planes, lines, MB, width), jnp.bfloat16),
            pltpu.VMEM((2, lines, MB, width), jnp.bfloat16),
            pltpu.VMEM((TERMS * MB, 6 * MB), jnp.bfloat16),
            pltpu.VMEM((planes + 2, lines, MB, width), jnp.float32),
            pltpu.VMEM((planes, lines, MB, width), jnp.float32),
            pltpu.VMEM((2, lines, MB, width), jnp.bfloat16),
            pltpu.VMEM((2, lines, MB, width), jnp.bfloat16),
            pltpu.SemaphoreType.DMA((flat // PIECE,)),
            pltpu.SemaphoreType.DMA((7,)),
            pltpu.SemaphoreType.DMA((9, 4)),
            pltpu.SemaphoreType.DMA((9, 4)),
            pltpu.SemaphoreType.REGULAR,
            pltpu.SemaphoreType.REGULAR,
            pltpu.SemaphoreType.REGULAR,
        ],
        compiler_params=pltpu.CompilerParams(
            collective_id=0, has_side_effects=True, vmem_limit_bytes=57 * 1024 * 1024
        ),
        cost_estimate=pl.CostEstimate(
            flops=2 * TERMS * 6 * MB * MB * species * planes * depth * width,
            bytes_accessed=2**21,
            transcendentals=0,
        ),
    )(
        section_field.reshape(flat, width),
        coupling.reshape(NNZ, TERMS, MB, MB),
        reaction_fields.reshape(K * planes * depth, width),
        block_list,
        diffusivity,
        species_mix,
        base_field.reshape(rows, STRIDE, width),
        prev_rate.reshape(rows, STRIDE, width),
    )
    rate = -minus_rate
    next_field = (held - half_step * minus_rate).astype(jnp.bfloat16)
    return (rate.reshape(section_field.shape), next_field.reshape(section_field.shape))


def solution(mesh):
    placed = (
        P("mode", None, "gx", None, None),
        P("mode", None, "gx", None, None),
        P("mode", None, "gx", None, None),
        P("mode", None),
        P("mode", None, None, None, None),
        P(),
        P(None, "gx", None, None),
        P(),
    )
    return jax.shard_map(
        shards,
        mesh=mesh,
        in_specs=placed,
        out_specs=(P("mode", None, "gx", None, None), P("mode", None, "gx", None, None)),
        check_vma=False,
    )
```

```python
import jax
import jax.numpy as jnp
from jax import lax
from jax.sharding import PartitionSpec as P
import jax.experimental.pallas as pl
import jax.experimental.pallas.tpu as pltpu

MB = 64
NBLK = 16
K = 4
TERMS = 1 + K
NNZ = 5
MESH = pl.DeviceIdType.MESH

half_step = 0.25

OWN, SIB, ACROSS, CROSS, RELAY, SIB2 = range(6)
TRANSIT, HALO_LO, HALO_HI = 6, 7, 8
PLANES = (3, 0, 1, 2)
PIECE = 512
STRIDE = 32


def kernel(
    section_hbm,
    coupling_hbm,
    fields_hbm,
    list_hbm,
    diffusivity_hbm,
    mix_hbm,
    base_hbm,
    prev_hbm,
    out_ref,
    held_ref,
    list_ref,
    diffusivity_ref,
    mix_ref,
    base,
    native,
    wide,
    couple,
    fields_in,
    fields,
    blocks,
    transit,
    weights,
    diff,
    react,
    edge,
    halo,
    own_sem,
    local_sem,
    send_sem,
    recv_sem,
    ready_sem,
    gather_sem,
    slabs_sem,
):
    g = lax.axis_index("gx")
    i = lax.axis_index("mode")
    y = i // 4
    h = lax.rem(i // 2, 2)
    c = lax.rem(i, 2)
    step = 1 - 2 * h

    def device(dy, hh, cc):
        return (g, lax.rem(y + dy + 4, 4) * 4 + hh * 2 + cc)

    at_cross = device(0, 1 - h, c)
    at_relay = device(step, h, c)
    at_back = device(-step, h, c)
    at_across = device(2, h, c)
    at_sib = device(0, h, 1 - c)
    flip = 1 - lax.rem(g, 2)
    at_up = (lax.rem(g + 17 - 2 * flip, 16), i)
    at_down = (lax.rem(g + 15 + 2 * flip, 16), i)

    def plane_of(plane):
        return plane + flip * (3 - 2 * plane)

    def signal(sem, peer):
        pl.semaphore_signal(sem, inc=1, device_id=peer, device_id_type=MESH)

    pieces = [pl.ds(n * PIECE, PIECE) for n in range(section_hbm.shape[0] // PIECE)]
    own = [
        pltpu.make_async_copy(section_hbm.at[rows], native.at[rows], own_sem.at[n])
        for n, rows in enumerate(pieces)
    ]
    for copy in own:
        copy.start()
    loads = [
        pltpu.make_async_copy(source, target, local_sem.at[n])
        for n, (source, target) in enumerate(
            (
                (coupling_hbm, couple),
                (fields_hbm, fields_in),
                (list_hbm, list_ref),
                (diffusivity_hbm, diffusivity_ref),
                (mix_hbm, mix_ref),
                (base_hbm, base),
                (prev_hbm, held_ref),
            )
        )
    ]

    first = y == 0
    second = y == 1
    barrier = pltpu.get_barrier_semaphore()

    @pl.when(jnp.logical_not(first))
    def _():
        signal(barrier, at_cross)
        signal(barrier, at_sib)

    for dy in (1, 2, 3):

        @pl.when(lax.rem(y + dy, 4) != 0)
        def _(dy=dy):
            signal(barrier, device(dy, h, c))

    @pl.when(first)
    def _():
        signal(barrier, device(1, 1 - h, c))
        signal(barrier, device(1, h, 1 - c))

    for copy in loads:
        copy.start()

    for copy, rows in zip(own, pieces):
        copy.wait()
        wide[rows, :] = native[rows, :].astype(jnp.float32)

    def arrange(pos):
        for sy in range(8):
            start = (sy // 4) * 16 + plane_of(PLANES[pos]) * 4 + sy % 4
            blocks[OWN, pos, sy] = wide[pl.ds(start, MB, stride=STRIDE), :].astype(jnp.bfloat16)

    arrange(0)
    arrange(1)

    @pl.when(second)
    def _():
        pl.semaphore_wait(barrier, 7)
        signal(ready_sem, device(3, h, c))

    @pl.when(y > 1)
    def _():
        pl.semaphore_wait(barrier, 5)
        signal(gather_sem, device(4 - y, h, c))

    @pl.when(first)
    def _():
        pl.semaphore_wait(ready_sem, 1)

    def send(kind, part, source, target, peer):
        return pltpu.make_async_remote_copy(
            src_ref=source,
            dst_ref=target,
            send_sem=send_sem.at[kind, part],
            recv_sem=recv_sem.at[kind, part],
            device_id=peer,
            device_id_type=MESH,
        )

    def block_send(source, target, pos, peer):
        return send(target, pos, blocks.at[source, pos], blocks.at[target, pos], peer)

    every = range(4)
    cross = [block_send(OWN, CROSS, p, at_cross) for p in every]
    relay = [block_send(CROSS, RELAY, p, at_relay) for p in every]
    back = [
        send(TRANSIT, p, blocks.at[OWN, p], transit.at[p - 2], at_back) for p in (2, 3)
    ]
    across = [block_send(OWN, ACROSS, p, at_across) for p in (0, 1)] + [
        send(ACROSS, p, transit.at[p - 2], blocks.at[ACROSS, p], at_back) for p in (2, 3)
    ]
    sib = send(SIB, 0, blocks.at[OWN], blocks.at[SIB], at_sib)
    sib_cross = [block_send(CROSS, SIB2, p, at_sib) for p in every]
    sib_relay = [block_send(RELAY, SIB2, p, at_sib) for p in every]
    halo_up = [
        send(HALO_HI, s, edge.at[0, pl.ds(4 * s, 4)], halo.at[1, pl.ds(4 * s, 4)], at_up)
        for s in (0, 1)
    ]
    halo_down = send(HALO_LO, 0, edge.at[1], halo.at[0], at_down)

    cross[0].start()
    across[0].start()
    cross[1].start()
    across[1].start()
    arrange(2)
    back[0].start()
    arrange(3)
    back[1].start()
    cross[2].start()
    cross[3].start()
    sib.start()

    @pl.when(first)
    def _():
        pl.semaphore_wait(gather_sem, 2)
        signal(barrier, at_up)
        signal(barrier, at_down)

    for copy in loads:
        copy.wait()
    fields[...] = fields_in[...].astype(jnp.float32)

    def chosen(target):
        target = lax.rem(target + NBLK, NBLK)
        total = None
        for n in range(1, NNZ - 1):
            keep = (list_ref[0, n] == target).astype(jnp.float32)
            term = keep * couple[n].astype(jnp.float32)
            total = term if total is None else total + term
        return total

    def side_by_side(first, second):
        pair = jnp.concatenate([first, second], axis=-1)
        return pair.reshape(TERMS * MB, 2 * MB).astype(jnp.bfloat16)

    weights[:, 0:128] = side_by_side(couple[0].astype(jnp.float32), chosen(i + 1 - 2 * c))
    weights[:, 128:256] = side_by_side(
        couple[NNZ - 1].astype(jnp.float32), chosen(i + 2 - 4 * h)
    )
    weights[:, 256:384] = side_by_side(chosen(i - 2 + 4 * h), chosen(i - 1 + 2 * c))

    @pl.loop(0, 8)
    def _(n):
        rows = pl.ds(n * 8, 8)
        held_ref[rows] = base[rows].astype(jnp.float32) + half_step * held_ref[rows]

    def multiply(pos, first, last, start=0, stop=4):
        plane = PLANES[pos]
        fresh = first == OWN

        @pl.loop(start, stop, unroll=stop - start)
        def _(n):
            sy = n * 2
            s = n // 2
            depth = (last - first) * MB
            sides = [blocks[first:last, pos, sy + k].reshape(depth, 128) for k in (0, 1)]
            result = jnp.dot(
                weights[:, first * MB : last * MB],
                jnp.concatenate(sides, axis=1),
                preferred_element_type=jnp.float32,
            )
            for k in (0, 1):
                columns = slice(128 * k, 128 * (k + 1))
                term_d = result[0:MB, columns]
                yy = lax.rem(sy, 4) + k
                row = plane_of(plane) * 4 + yy
                term_r = fields[pl.ds(row, 1), :] * result[MB : 2 * MB, columns]
                for t in range(1, K):
                    term_r = term_r + fields[pl.ds(16 * t + row, 1), :] * result[
                        (1 + t) * MB : (2 + t) * MB, columns
                    ]
                if fresh:
                    mixed = mix_ref[s, 0] * blocks[OWN, pos, yy].astype(jnp.float32)
                    mixed = mixed + mix_ref[s, 1] * blocks[OWN, pos, 4 + yy].astype(jnp.float32)
                    diff[1 + plane, sy + k] = term_d
                    react[plane, sy + k] = term_r - mixed
                else:
                    total = diff[1 + plane, sy + k] + term_d
                    diff[1 + plane, sy + k] = total
                    react[plane, sy + k] += term_r
                    if pos < 2:
                        edge[pos, sy + k] = total.astype(jnp.bfloat16)

    def in_plane(plane, sy):
        s4 = (sy // 4) * 4
        center = diff[1 + plane, sy]
        lap = diff[1 + plane, s4 + (sy + 1) % 4] + diff[1 + plane, s4 + (sy + 3) % 4]
        lap = lap + (pltpu.roll(center, 1, 1) + pltpu.roll(center, 127, 1))
        return lap - 6.0 * center

    def pass_on(copies, yes, p):
        @pl.when(yes)
        def _():
            copies[p].start()

    def take_cross(p):
        cross[p].wait_recv()
        relay[p].start()
        pass_on(sib_cross, c == h, p)

    def take_relay(p):
        relay[p].wait_recv()
        pass_on(sib_relay, c != h, p)

    def late(pos):
        sib_cross[pos].wait_recv()
        multiply(pos, RELAY, SIB2 + 1)

    def lessen(plane, others):
        for sy in range(8):
            part = in_plane(plane, sy)
            for other in others:
                part = part + diff[1 + other, sy]
            react[plane, sy] -= diffusivity_ref[sy // 4] * part

    def finish(pair):
        for flipped in (0, 1):
            planes = (2 * pair + 1, 2 * pair) if flipped else (2 * pair, 2 * pair + 1)

            @pl.when(flip == flipped)
            def _(planes=planes, block=1 - pair if flipped else pair):
                finish_block(planes, block)

    def finish_block(planes, block):
        @pl.loop(0, MB // 16, unroll=4)
        def _(n):
            rows = pl.ds(pl.multiple_of(16 * n, 16), 16)

            def at(plane, sy):
                return diff[1 + plane, sy, rows, :]

            def in_plane_rows(plane, sy):
                s4 = (sy // 4) * 4
                center = at(plane, sy)
                lap = at(plane, s4 + (sy + 1) % 4) + at(plane, s4 + (sy + 3) % 4)
                lap = lap + (pltpu.roll(center, 1, 1) + pltpu.roll(center, 127, 1))
                return lap - 6.0 * center

            for s in range(2):
                lines = []
                for plane in planes:
                    for sy in range(4 * s, 4 * s + 4):
                        if plane == 0:
                            part = at(1, sy) + halo[0, sy, rows, :].astype(jnp.float32)
                        elif plane == 1:
                            part = at(2, sy)
                        elif plane == 2:
                            part = in_plane_rows(2, sy) + (at(1, sy) + at(3, sy))
                        else:
                            part = at(2, sy) + halo[1, sy, rows, :].astype(jnp.float32)
                        lines.append(diffusivity_ref[s] * part - react[plane, sy, rows, :])
                out_ref[rows, pl.ds(8 * (2 * s + block), 8), :] = jnp.swapaxes(
                    jnp.stack(lines, axis=0), 0, 1
                )

    take_cross(0)
    take_cross(1)
    back[0].wait_recv()
    across[2].start()
    sib.wait_recv()
    across[0].wait_recv()
    multiply(0, OWN, RELAY)
    take_relay(0)

    @pl.when(first)
    def _():
        pl.semaphore_wait(barrier, 2)
        for dy in (1, 2, 3):
            signal(slabs_sem, device(dy, h, c))

    sib_cross[0].wait_recv()
    multiply(0, RELAY, SIB2 + 1, 0, 2)

    @pl.when(jnp.logical_not(first))
    def _():
        pl.semaphore_wait(slabs_sem, 1)

    halo_up[0].start()
    multiply(0, RELAY, SIB2 + 1, 2, 4)
    halo_up[1].start()
    take_cross(2)
    across[1].wait_recv()
    multiply(1, OWN, RELAY)
    back[1].wait_recv()
    across[3].start()
    take_cross(3)
    take_relay(1)
    lessen(3, ())
    late(1)
    halo_down.start()
    lessen(0, ())
    across[2].wait_recv()
    multiply(2, OWN, RELAY)
    take_relay(2)
    late(2)
    lessen(1, (0,))
    across[3].wait_recv()
    multiply(3, OWN, RELAY)
    take_relay(3)
    late(3)
    halo_down.wait_recv()
    finish(0)
    for copy in halo_up:
        copy.wait_recv()
    finish(1)

    for copy in (*cross, *relay, *back, *across, sib, *sib_cross, *halo_up, halo_down):
        copy.wait_send()


def last_kernel(rate_ref, held_ref, rate_hbm, next_hbm, after, rate_sem, next_sem):
    leave = pltpu.make_async_copy(rate_ref, rate_hbm, rate_sem)
    leave.start()
    size = MB // 2
    copies = []
    for n in range(2):
        rows = pl.ds(n * size, size)
        after[rows] = (held_ref[rows] + half_step * rate_ref[rows]).astype(jnp.bfloat16)
        copies.append(pltpu.make_async_copy(after.at[rows], next_hbm.at[rows], next_sem.at[n]))
        copies[-1].start()
    for copy in copies:
        copy.wait()
    leave.wait()


def shards(
    section_field,
    base_field,
    prev_rate,
    block_list,
    coupling,
    diffusivity,
    reaction_fields,
    species_mix,
):
    rows, species, planes, depth, width = section_field.shape
    flat = rows * species * planes * depth
    lines = species * depth
    in_hbm = pl.BlockSpec(memory_space=pltpu.HBM)
    in_vmem = pl.BlockSpec(memory_space=pltpu.VMEM)
    rate, held = pl.pallas_call(
        kernel,
        name="galerkin",
        out_shape=(
            pltpu.VMEM((rows, STRIDE, width), jnp.float32),
            pltpu.VMEM((rows, STRIDE, width), jnp.float32),
        ),
        in_specs=[in_hbm] * 8,
        out_specs=(in_vmem, in_vmem),
        scratch_shapes=[
            pltpu.SMEM(block_list.shape, block_list.dtype),
            pltpu.SMEM(diffusivity.shape, diffusivity.dtype),
            pltpu.SMEM(species_mix.shape, species_mix.dtype),
            pltpu.VMEM((rows, STRIDE, width), jnp.bfloat16),
            pltpu.VMEM((flat, width), jnp.bfloat16),
            pltpu.VMEM((flat, width), jnp.float32),
            pltpu.VMEM((NNZ, TERMS, MB, MB), jnp.bfloat16),
            pltpu.VMEM((K * planes * depth, width), jnp.bfloat16),
            pltpu.VMEM((K * planes * depth, width), jnp.float32),
            pltpu.VMEM((6, planes, lines, MB, width), jnp.bfloat16),
            pltpu.VMEM((2, lines, MB, width), jnp.bfloat16),
            pltpu.VMEM((TERMS * MB, 6 * MB), jnp.bfloat16),
            pltpu.VMEM((planes + 2, lines, MB, width), jnp.float32),
            pltpu.VMEM((planes, lines, MB, width), jnp.float32),
            pltpu.VMEM((2, lines, MB, width), jnp.bfloat16),
            pltpu.VMEM((2, lines, MB, width), jnp.bfloat16),
            pltpu.SemaphoreType.DMA((flat // PIECE,)),
            pltpu.SemaphoreType.DMA((7,)),
            pltpu.SemaphoreType.DMA((9, 4)),
            pltpu.SemaphoreType.DMA((9, 4)),
            pltpu.SemaphoreType.REGULAR,
            pltpu.SemaphoreType.REGULAR,
            pltpu.SemaphoreType.REGULAR,
        ],
        compiler_params=pltpu.CompilerParams(
            collective_id=0, has_side_effects=True, vmem_limit_bytes=57 * 1024 * 1024
        ),
        cost_estimate=pl.CostEstimate(
            flops=2 * TERMS * 6 * MB * MB * species * planes * depth * width,
            bytes_accessed=2**21,
            transcendentals=0,
        ),
    )(
        section_field.reshape(flat, width),
        coupling.reshape(NNZ, TERMS, MB, MB),
        reaction_fields.reshape(K * planes * depth, width),
        block_list,
        diffusivity,
        species_mix,
        base_field.reshape(rows, STRIDE, width),
        prev_rate.reshape(rows, STRIDE, width),
    )
    rate, next_field = pl.pallas_call(
        last_kernel,
        name="next_section",
        out_shape=(
            jax.ShapeDtypeStruct((rows, STRIDE, width), jnp.float32),
            jax.ShapeDtypeStruct((rows, STRIDE, width), jnp.bfloat16),
        ),
        in_specs=[in_vmem] * 2,
        out_specs=[in_hbm] * 2,
        scratch_shapes=[
            pltpu.VMEM((rows, STRIDE, width), jnp.bfloat16),
            pltpu.SemaphoreType.DMA,
            pltpu.SemaphoreType.DMA((2,)),
        ],
        compiler_params=pltpu.CompilerParams(vmem_limit_bytes=16 * 1024 * 1024),
    )(rate, held)
    return (rate.reshape(section_field.shape), next_field.reshape(section_field.shape))


def solution(mesh):
    placed = (
        P("mode", None, "gx", None, None),
        P("mode", None, "gx", None, None),
        P("mode", None, "gx", None, None),
        P("mode", None),
        P("mode", None, None, None, None),
        P(),
        P(None, "gx", None, None),
        P(),
    )
    return jax.shard_map(
        shards,
        mesh=mesh,
        in_specs=placed,
        out_specs=(P("mode", None, "gx", None, None), P("mode", None, "gx", None, None)),
        check_vma=False,
    )
```

```python
import jax
import jax.numpy as jnp
from jax import lax
from jax.sharding import PartitionSpec as P
import jax.experimental.pallas as pl
import jax.experimental.pallas.tpu as pltpu

MB = 64
NBLK = 16
K = 4
TERMS = 1 + K
NNZ = 5
MESH = pl.DeviceIdType.MESH

half_step = 0.25

OWN, SIB, ACROSS, CROSS, RELAY, SIB2 = range(6)
TRANSIT, HALO_LO, HALO_HI = 6, 7, 8
PLANES = (3, 0, 1, 2)
PIECE = 512
STRIDE = 32


def kernel(
    section_hbm,
    coupling_hbm,
    fields_hbm,
    list_hbm,
    diffusivity_hbm,
    mix_hbm,
    base_hbm,
    prev_hbm,
    out_ref,
    held_ref,
    list_ref,
    diffusivity_ref,
    mix_ref,
    base,
    native,
    wide,
    couple,
    fields_in,
    fields,
    blocks,
    transit,
    weights,
    diff,
    react,
    edge,
    halo,
    own_sem,
    local_sem,
    send_sem,
    recv_sem,
    ready_sem,
    gather_sem,
    slabs_sem,
):
    g = lax.axis_index("gx")
    i = lax.axis_index("mode")
    y = i // 4
    h = lax.rem(i // 2, 2)
    c = lax.rem(i, 2)
    step = 1 - 2 * h

    def device(dy, hh, cc):
        return (g, lax.rem(y + dy + 4, 4) * 4 + hh * 2 + cc)

    at_cross = device(0, 1 - h, c)
    at_relay = device(step, h, c)
    at_back = device(-step, h, c)
    at_across = device(2, h, c)
    at_sib = device(0, h, 1 - c)
    flip = 1 - lax.rem(g, 2)
    at_up = (lax.rem(g + 17 - 2 * flip, 16), i)
    at_down = (lax.rem(g + 15 + 2 * flip, 16), i)

    def plane_of(plane):
        return plane + flip * (3 - 2 * plane)

    def signal(sem, peer):
        pl.semaphore_signal(sem, inc=1, device_id=peer, device_id_type=MESH)

    pieces = [pl.ds(n * PIECE, PIECE) for n in range(section_hbm.shape[0] // PIECE)]
    own = [
        pltpu.make_async_copy(section_hbm.at[rows], native.at[rows], own_sem.at[n])
        for n, rows in enumerate(pieces)
    ]
    for copy in own:
        copy.start()
    loads = [
        pltpu.make_async_copy(source, target, local_sem.at[n])
        for n, (source, target) in enumerate(
            (
                (coupling_hbm, couple),
                (fields_hbm, fields_in),
                (list_hbm, list_ref),
                (diffusivity_hbm, diffusivity_ref),
                (mix_hbm, mix_ref),
                (base_hbm, base),
                (prev_hbm, held_ref),
            )
        )
    ]

    first = y == 0
    second = y == 1
    barrier = pltpu.get_barrier_semaphore()

    @pl.when(jnp.logical_not(first))
    def _():
        signal(barrier, at_cross)
        signal(barrier, at_sib)

    for dy in (1, 2, 3):

        @pl.when(lax.rem(y + dy, 4) != 0)
        def _(dy=dy):
            signal(barrier, device(dy, h, c))

    @pl.when(first)
    def _():
        signal(barrier, device(1, 1 - h, c))
        signal(barrier, device(1, h, 1 - c))

    for copy in loads:
        copy.start()

    for copy, rows in zip(own, pieces):
        copy.wait()
        wide[rows, :] = native[rows, :].astype(jnp.float32)

    def arrange(pos):
        for sy in range(8):
            start = (sy // 4) * 16 + plane_of(PLANES[pos]) * 4 + sy % 4
            blocks[OWN, pos, sy] = wide[pl.ds(start, MB, stride=STRIDE), :].astype(jnp.bfloat16)

    arrange(0)
    arrange(1)

    @pl.when(second)
    def _():
        pl.semaphore_wait(barrier, 7)
        signal(ready_sem, device(3, h, c))

    @pl.when(y > 1)
    def _():
        pl.semaphore_wait(barrier, 5)
        signal(gather_sem, device(4 - y, h, c))

    @pl.when(first)
    def _():
        pl.semaphore_wait(ready_sem, 1)

    def send(kind, part, source, target, peer):
        return pltpu.make_async_remote_copy(
            src_ref=source,
            dst_ref=target,
            send_sem=send_sem.at[kind, part],
            recv_sem=recv_sem.at[kind, part],
            device_id=peer,
            device_id_type=MESH,
        )

    def block_send(source, target, pos, peer):
        return send(target, pos, blocks.at[source, pos], blocks.at[target, pos], peer)

    every = range(4)
    cross = [block_send(OWN, CROSS, p, at_cross) for p in every]
    relay = [block_send(CROSS, RELAY, p, at_relay) for p in every]
    back = [
        send(TRANSIT, p, blocks.at[OWN, p], transit.at[p - 2], at_back) for p in (2, 3)
    ]
    across = [block_send(OWN, ACROSS, p, at_across) for p in (0, 1)] + [
        send(ACROSS, p, transit.at[p - 2], blocks.at[ACROSS, p], at_back) for p in (2, 3)
    ]
    sib = send(SIB, 0, blocks.at[OWN], blocks.at[SIB], at_sib)
    sib_cross = [block_send(CROSS, SIB2, p, at_sib) for p in every]
    sib_relay = [block_send(RELAY, SIB2, p, at_sib) for p in every]
    halo_up = send(HALO_HI, 0, edge.at[0], halo.at[1], at_up)
    halo_down = send(HALO_LO, 0, edge.at[1], halo.at[0], at_down)

    cross[0].start()
    across[0].start()
    cross[1].start()
    across[1].start()
    arrange(2)
    back[0].start()
    arrange(3)
    back[1].start()
    cross[2].start()
    cross[3].start()
    sib.start()

    @pl.when(first)
    def _():
        pl.semaphore_wait(gather_sem, 2)
        signal(barrier, at_up)
        signal(barrier, at_down)

    for copy in loads:
        copy.wait()
    fields[...] = fields_in[...].astype(jnp.float32)

    def chosen(target):
        target = lax.rem(target + NBLK, NBLK)
        total = None
        for n in range(1, NNZ - 1):
            keep = (list_ref[0, n] == target).astype(jnp.float32)
            term = keep * couple[n].astype(jnp.float32)
            total = term if total is None else total + term
        return total

    def side_by_side(first, second):
        pair = jnp.concatenate([first, second], axis=-1)
        return pair.reshape(TERMS * MB, 2 * MB).astype(jnp.bfloat16)

    weights[:, 0:128] = side_by_side(couple[0].astype(jnp.float32), chosen(i + 1 - 2 * c))
    weights[:, 128:256] = side_by_side(
        couple[NNZ - 1].astype(jnp.float32), chosen(i + 2 - 4 * h)
    )
    weights[:, 256:384] = side_by_side(chosen(i - 2 + 4 * h), chosen(i - 1 + 2 * c))

    @pl.loop(0, 8)
    def _(n):
        rows = pl.ds(n * 8, 8)
        held_ref[rows] = base[rows].astype(jnp.float32) + half_step * held_ref[rows]

    def multiply(pos, first, last):
        plane = PLANES[pos]
        fresh = first == OWN

        @pl.loop(0, 4, unroll=4)
        def _(n):
            sy = n * 2
            s = n // 2
            depth = (last - first) * MB
            sides = [blocks[first:last, pos, sy + k].reshape(depth, 128) for k in (0, 1)]
            result = jnp.dot(
                weights[:, first * MB : last * MB],
                jnp.concatenate(sides, axis=1),
                preferred_element_type=jnp.float32,
            )
            for k in (0, 1):
                columns = slice(128 * k, 128 * (k + 1))
                term_d = result[0:MB, columns]
                yy = lax.rem(sy, 4) + k
                row = plane_of(plane) * 4 + yy
                term_r = fields[pl.ds(row, 1), :] * result[MB : 2 * MB, columns]
                for t in range(1, K):
                    term_r = term_r + fields[pl.ds(16 * t + row, 1), :] * result[
                        (1 + t) * MB : (2 + t) * MB, columns
                    ]
                if fresh:
                    mixed = mix_ref[s, 0] * blocks[OWN, pos, yy].astype(jnp.float32)
                    mixed = mixed + mix_ref[s, 1] * blocks[OWN, pos, 4 + yy].astype(jnp.float32)
                    diff[1 + plane, sy + k] = term_d
                    react[plane, sy + k] = term_r - mixed
                else:
                    total = diff[1 + plane, sy + k] + term_d
                    diff[1 + plane, sy + k] = total
                    react[plane, sy + k] += term_r
                    if pos < 2:
                        edge[pos, sy + k] = total.astype(jnp.bfloat16)

    def in_plane(plane, sy):
        s4 = (sy // 4) * 4
        center = diff[1 + plane, sy]
        lap = diff[1 + plane, s4 + (sy + 1) % 4] + diff[1 + plane, s4 + (sy + 3) % 4]
        lap = lap + (pltpu.roll(center, 1, 1) + pltpu.roll(center, 127, 1))
        return lap - 6.0 * center

    def pass_on(copies, yes, p):
        @pl.when(yes)
        def _():
            copies[p].start()

    def take_cross(p):
        cross[p].wait_recv()
        relay[p].start()
        pass_on(sib_cross, c == h, p)

    def take_relay(p):
        relay[p].wait_recv()
        pass_on(sib_relay, c != h, p)

    def late(pos):
        sib_cross[pos].wait_recv()
        multiply(pos, RELAY, SIB2 + 1)

    def lessen(plane, others):
        for sy in range(8):
            part = in_plane(plane, sy)
            for other in others:
                part = part + diff[1 + other, sy]
            react[plane, sy] -= diffusivity_ref[sy // 4] * part

    def finish(pair):
        for flipped in (0, 1):
            planes = (2 * pair + 1, 2 * pair) if flipped else (2 * pair, 2 * pair + 1)

            @pl.when(flip == flipped)
            def _(planes=planes, block=1 - pair if flipped else pair):
                finish_block(planes, block)

    def finish_block(planes, block):
        @pl.loop(0, MB // 16, unroll=4)
        def _(n):
            rows = pl.ds(pl.multiple_of(16 * n, 16), 16)

            def at(plane, sy):
                return diff[1 + plane, sy, rows, :]

            def in_plane_rows(plane, sy):
                s4 = (sy // 4) * 4
                center = at(plane, sy)
                lap = at(plane, s4 + (sy + 1) % 4) + at(plane, s4 + (sy + 3) % 4)
                lap = lap + (pltpu.roll(center, 1, 1) + pltpu.roll(center, 127, 1))
                return lap - 6.0 * center

            for s in range(2):
                lines = []
                for plane in planes:
                    for sy in range(4 * s, 4 * s + 4):
                        if plane == 0:
                            part = at(1, sy) + halo[0, sy, rows, :].astype(jnp.float32)
                        elif plane == 1:
                            part = at(2, sy)
                        elif plane == 2:
                            part = in_plane_rows(2, sy) + (at(1, sy) + at(3, sy))
                        else:
                            part = at(2, sy) + halo[1, sy, rows, :].astype(jnp.float32)
                        lines.append(diffusivity_ref[s] * part - react[plane, sy, rows, :])
                out_ref[rows, pl.ds(8 * (2 * s + block), 8), :] = jnp.swapaxes(
                    jnp.stack(lines, axis=0), 0, 1
                )

    take_cross(0)
    take_cross(1)
    back[0].wait_recv()
    across[2].start()
    sib.wait_recv()
    across[0].wait_recv()
    multiply(0, OWN, RELAY)
    take_relay(0)

    @pl.when(first)
    def _():
        pl.semaphore_wait(barrier, 2)
        for dy in (1, 2, 3):
            signal(slabs_sem, device(dy, h, c))

    late(0)

    @pl.when(jnp.logical_not(first))
    def _():
        pl.semaphore_wait(slabs_sem, 1)

    halo_up.start()
    take_cross(2)
    across[1].wait_recv()
    multiply(1, OWN, RELAY)
    back[1].wait_recv()
    across[3].start()
    take_cross(3)
    take_relay(1)
    lessen(3, ())
    late(1)
    halo_down.start()
    lessen(0, ())
    across[2].wait_recv()
    multiply(2, OWN, RELAY)
    take_relay(2)
    late(2)
    lessen(1, (0,))
    across[3].wait_recv()
    multiply(3, OWN, RELAY)
    take_relay(3)
    late(3)
    halo_down.wait_recv()
    finish(0)
    halo_up.wait_recv()
    finish(1)

    for copy in (*cross, *relay, *back, *across, sib, *sib_cross, halo_up, halo_down):
        copy.wait_send()


def last_kernel(rate_ref, held_ref, rate_hbm, next_hbm, after, rate_sem, next_sem):
    leave = pltpu.make_async_copy(rate_ref, rate_hbm, rate_sem)
    leave.start()
    size = MB // 2
    copies = []
    for n in range(2):
        rows = pl.ds(n * size, size)
        after[rows] = (held_ref[rows] + half_step * rate_ref[rows]).astype(jnp.bfloat16)
        copies.append(pltpu.make_async_copy(after.at[rows], next_hbm.at[rows], next_sem.at[n]))
        copies[-1].start()
    for copy in copies:
        copy.wait()
    leave.wait()


def shards(
    section_field,
    base_field,
    prev_rate,
    block_list,
    coupling,
    diffusivity,
    reaction_fields,
    species_mix,
):
    rows, species, planes, depth, width = section_field.shape
    flat = rows * species * planes * depth
    lines = species * depth
    in_hbm = pl.BlockSpec(memory_space=pltpu.HBM)
    in_vmem = pl.BlockSpec(memory_space=pltpu.VMEM)
    rate, held = pl.pallas_call(
        kernel,
        name="galerkin",
        out_shape=(
            pltpu.VMEM((rows, STRIDE, width), jnp.float32),
            pltpu.VMEM((rows, STRIDE, width), jnp.float32),
        ),
        in_specs=[in_hbm] * 8,
        out_specs=(in_vmem, in_vmem),
        scratch_shapes=[
            pltpu.SMEM(block_list.shape, block_list.dtype),
            pltpu.SMEM(diffusivity.shape, diffusivity.dtype),
            pltpu.SMEM(species_mix.shape, species_mix.dtype),
            pltpu.VMEM((rows, STRIDE, width), jnp.bfloat16),
            pltpu.VMEM((flat, width), jnp.bfloat16),
            pltpu.VMEM((flat, width), jnp.float32),
            pltpu.VMEM((NNZ, TERMS, MB, MB), jnp.bfloat16),
            pltpu.VMEM((K * planes * depth, width), jnp.bfloat16),
            pltpu.VMEM((K * planes * depth, width), jnp.float32),
            pltpu.VMEM((6, planes, lines, MB, width), jnp.bfloat16),
            pltpu.VMEM((2, lines, MB, width), jnp.bfloat16),
            pltpu.VMEM((TERMS * MB, 6 * MB), jnp.bfloat16),
            pltpu.VMEM((planes + 2, lines, MB, width), jnp.float32),
            pltpu.VMEM((planes, lines, MB, width), jnp.float32),
            pltpu.VMEM((2, lines, MB, width), jnp.bfloat16),
            pltpu.VMEM((2, lines, MB, width), jnp.bfloat16),
            pltpu.SemaphoreType.DMA((flat // PIECE,)),
            pltpu.SemaphoreType.DMA((7,)),
            pltpu.SemaphoreType.DMA((9, 4)),
            pltpu.SemaphoreType.DMA((9, 4)),
            pltpu.SemaphoreType.REGULAR,
            pltpu.SemaphoreType.REGULAR,
            pltpu.SemaphoreType.REGULAR,
        ],
        compiler_params=pltpu.CompilerParams(
            collective_id=0, has_side_effects=True, vmem_limit_bytes=57 * 1024 * 1024
        ),
        cost_estimate=pl.CostEstimate(
            flops=2 * TERMS * 6 * MB * MB * species * planes * depth * width,
            bytes_accessed=2**21,
            transcendentals=0,
        ),
    )(
        section_field.reshape(flat, width),
        coupling.reshape(NNZ, TERMS, MB, MB),
        reaction_fields.reshape(K * planes * depth, width),
        block_list,
        diffusivity,
        species_mix,
        base_field.reshape(rows, STRIDE, width),
        prev_rate.reshape(rows, STRIDE, width),
    )
    rate, next_field = pl.pallas_call(
        last_kernel,
        name="next_section",
        out_shape=(
            jax.ShapeDtypeStruct((rows, STRIDE, width), jnp.float32),
            jax.ShapeDtypeStruct((rows, STRIDE, width), jnp.bfloat16),
        ),
        in_specs=[in_vmem] * 2,
        out_specs=[in_hbm] * 2,
        scratch_shapes=[
            pltpu.VMEM((rows, STRIDE, width), jnp.bfloat16),
            pltpu.SemaphoreType.DMA,
            pltpu.SemaphoreType.DMA((2,)),
        ],
        compiler_params=pltpu.CompilerParams(vmem_limit_bytes=16 * 1024 * 1024),
    )(rate, held)
    return (rate.reshape(section_field.shape), next_field.reshape(section_field.shape))


def solution(mesh):
    placed = (
        P("mode", None, "gx", None, None),
        P("mode", None, "gx", None, None),
        P("mode", None, "gx", None, None),
        P("mode", None),
        P("mode", None, None, None, None),
        P(),
        P(None, "gx", None, None),
        P(),
    )
    return jax.shard_map(
        shards,
        mesh=mesh,
        in_specs=placed,
        out_specs=(P("mode", None, "gx", None, None), P("mode", None, "gx", None, None)),
        check_vma=False,
    )
```

```python
import jax
import jax.numpy as jnp
from jax import lax
from jax.sharding import PartitionSpec as P
import jax.experimental.pallas as pl
import jax.experimental.pallas.tpu as pltpu

MB = 64
NBLK = 16
K = 4
TERMS = 1 + K
NNZ = 5
MESH = pl.DeviceIdType.MESH

half_step = 0.25

OWN, SIB, ACROSS, CROSS, RELAY, SIB2 = range(6)
TRANSIT, HALO_LO, HALO_HI = 6, 7, 8
PLANES = (3, 0, 1, 2)
PIECE = 512
STRIDE = 32


def kernel(
    section_hbm,
    coupling_hbm,
    fields_hbm,
    list_hbm,
    diffusivity_hbm,
    mix_hbm,
    base_hbm,
    prev_hbm,
    out_ref,
    held_ref,
    list_ref,
    diffusivity_ref,
    mix_ref,
    base,
    native,
    wide,
    couple,
    fields_in,
    fields,
    blocks,
    transit,
    weights,
    diff,
    react,
    edge,
    halo,
    own_sem,
    local_sem,
    send_sem,
    recv_sem,
    ready_sem,
    gather_sem,
    slabs_sem,
):
    g = lax.axis_index("gx")
    i = lax.axis_index("mode")
    y = i // 4
    h = lax.rem(i // 2, 2)
    c = lax.rem(i, 2)
    step = 1 - 2 * h

    def device(dy, hh, cc):
        return (g, lax.rem(y + dy + 4, 4) * 4 + hh * 2 + cc)

    at_cross = device(0, 1 - h, c)
    at_relay = device(step, h, c)
    at_back = device(-step, h, c)
    at_across = device(2, h, c)
    at_sib = device(0, h, 1 - c)
    flip = 1 - lax.rem(g, 2)
    at_up = (lax.rem(g + 17 - 2 * flip, 16), i)
    at_down = (lax.rem(g + 15 + 2 * flip, 16), i)

    def plane_of(plane):
        return plane + flip * (3 - 2 * plane)

    def signal(sem, peer):
        pl.semaphore_signal(sem, inc=1, device_id=peer, device_id_type=MESH)

    pieces = [pl.ds(n * PIECE, PIECE) for n in range(section_hbm.shape[0] // PIECE)]
    own = [
        pltpu.make_async_copy(section_hbm.at[rows], native.at[rows], own_sem.at[n])
        for n, rows in enumerate(pieces)
    ]
    for copy in own:
        copy.start()
    loads = [
        pltpu.make_async_copy(source, target, local_sem.at[n])
        for n, (source, target) in enumerate(
            (
                (coupling_hbm, couple),
                (fields_hbm, fields_in),
                (list_hbm, list_ref),
                (diffusivity_hbm, diffusivity_ref),
                (mix_hbm, mix_ref),
                (base_hbm, base),
                (prev_hbm, held_ref),
            )
        )
    ]

    first = y == 0
    second = y == 1
    barrier = pltpu.get_barrier_semaphore()

    @pl.when(jnp.logical_not(first))
    def _():
        signal(barrier, at_cross)
        signal(barrier, at_sib)

    for dy in (1, 2, 3):

        @pl.when(lax.rem(y + dy, 4) != 0)
        def _(dy=dy):
            signal(barrier, device(dy, h, c))

    @pl.when(first)
    def _():
        signal(barrier, device(1, 1 - h, c))
        signal(barrier, device(1, h, 1 - c))

    for copy in loads:
        copy.start()

    for copy, rows in zip(own, pieces):
        copy.wait()
        wide[rows, :] = native[rows, :].astype(jnp.float32)

    def arrange(pos):
        for sy in range(8):
            start = (sy // 4) * 16 + plane_of(PLANES[pos]) * 4 + sy % 4
            blocks[OWN, pos, sy] = wide[pl.ds(start, MB, stride=STRIDE), :].astype(jnp.bfloat16)

    arrange(0)
    arrange(1)

    @pl.when(second)
    def _():
        pl.semaphore_wait(barrier, 7)
        signal(ready_sem, device(3, h, c))

    @pl.when(y > 1)
    def _():
        pl.semaphore_wait(barrier, 5)
        signal(gather_sem, device(4 - y, h, c))

    @pl.when(first)
    def _():
        pl.semaphore_wait(ready_sem, 1)

    def send(kind, part, source, target, peer):
        return pltpu.make_async_remote_copy(
            src_ref=source,
            dst_ref=target,
            send_sem=send_sem.at[kind, part],
            recv_sem=recv_sem.at[kind, part],
            device_id=peer,
            device_id_type=MESH,
        )

    def block_send(source, target, pos, peer):
        return send(target, pos, blocks.at[source, pos], blocks.at[target, pos], peer)

    every = range(4)
    cross = [block_send(OWN, CROSS, p, at_cross) for p in every]
    relay = [block_send(CROSS, RELAY, p, at_relay) for p in every]
    back = [
        send(TRANSIT, p, blocks.at[OWN, p], transit.at[p - 2], at_back) for p in (2, 3)
    ]
    across = [block_send(OWN, ACROSS, p, at_across) for p in (0, 1)] + [
        send(ACROSS, p, transit.at[p - 2], blocks.at[ACROSS, p], at_back) for p in (2, 3)
    ]
    sib = send(SIB, 0, blocks.at[OWN], blocks.at[SIB], at_sib)
    sib_cross = [block_send(CROSS, SIB2, p, at_sib) for p in every]
    sib_relay = [block_send(RELAY, SIB2, p, at_sib) for p in every]
    halo_up = send(HALO_HI, 0, edge.at[0], halo.at[1], at_up)
    halo_down = send(HALO_LO, 0, edge.at[1], halo.at[0], at_down)

    cross[0].start()
    across[0].start()
    cross[1].start()
    across[1].start()
    arrange(2)
    back[0].start()
    arrange(3)
    back[1].start()
    cross[2].start()
    cross[3].start()
    sib.start()

    @pl.when(first)
    def _():
        pl.semaphore_wait(gather_sem, 2)
        signal(barrier, at_up)
        signal(barrier, at_down)

    for copy in loads:
        copy.wait()
    fields[...] = fields_in[...].astype(jnp.float32)

    def chosen(target):
        target = lax.rem(target + NBLK, NBLK)
        total = None
        for n in range(1, NNZ - 1):
            keep = (list_ref[0, n] == target).astype(jnp.float32)
            term = keep * couple[n].astype(jnp.float32)
            total = term if total is None else total + term
        return total

    def side_by_side(first, second):
        pair = jnp.concatenate([first, second], axis=-1)
        return pair.reshape(TERMS * MB, 2 * MB).astype(jnp.bfloat16)

    weights[:, 0:128] = side_by_side(couple[0].astype(jnp.float32), chosen(i + 1 - 2 * c))
    weights[:, 128:256] = side_by_side(
        couple[NNZ - 1].astype(jnp.float32), chosen(i + 2 - 4 * h)
    )
    weights[:, 256:384] = side_by_side(chosen(i - 2 + 4 * h), chosen(i - 1 + 2 * c))

    @pl.loop(0, 8)
    def _(n):
        rows = pl.ds(n * 8, 8)
        held_ref[rows] = base[rows].astype(jnp.float32) + half_step * held_ref[rows]

    def multiply(pos, first, last):
        plane = PLANES[pos]
        fresh = first == OWN

        @pl.loop(0, 4, unroll=4)
        def _(n):
            sy = n * 2
            s = n // 2
            depth = (last - first) * MB
            sides = [blocks[first:last, pos, sy + k].reshape(depth, 128) for k in (0, 1)]
            result = jnp.dot(
                weights[:, first * MB : last * MB],
                jnp.concatenate(sides, axis=1),
                preferred_element_type=jnp.float32,
            )
            for k in (0, 1):
                columns = slice(128 * k, 128 * (k + 1))
                term_d = result[0:MB, columns]
                yy = lax.rem(sy, 4) + k
                row = plane_of(plane) * 4 + yy
                term_r = fields[pl.ds(row, 1), :] * result[MB : 2 * MB, columns]
                for t in range(1, K):
                    term_r = term_r + fields[pl.ds(16 * t + row, 1), :] * result[
                        (1 + t) * MB : (2 + t) * MB, columns
                    ]
                if fresh:
                    mixed = mix_ref[s, 0] * blocks[OWN, pos, yy].astype(jnp.float32)
                    mixed = mixed + mix_ref[s, 1] * blocks[OWN, pos, 4 + yy].astype(jnp.float32)
                    diff[1 + plane, sy + k] = term_d
                    react[plane, sy + k] = term_r - mixed
                else:
                    total = diff[1 + plane, sy + k] + term_d
                    diff[1 + plane, sy + k] = total
                    react[plane, sy + k] += term_r
                    if pos < 2:
                        edge[pos, sy + k] = total.astype(jnp.bfloat16)

    def in_plane(plane, sy):
        s4 = (sy // 4) * 4
        center = diff[1 + plane, sy]
        lap = diff[1 + plane, s4 + (sy + 1) % 4] + diff[1 + plane, s4 + (sy + 3) % 4]
        lap = lap + (pltpu.roll(center, 1, 1) + pltpu.roll(center, 127, 1))
        return lap - 6.0 * center

    def pass_on(copies, yes, p):
        @pl.when(yes)
        def _():
            copies[p].start()

    def take_cross(p):
        cross[p].wait_recv()
        relay[p].start()
        pass_on(sib_cross, c == h, p)

    def take_relay(p):
        relay[p].wait_recv()
        pass_on(sib_relay, c != h, p)

    def late(pos):
        sib_cross[pos].wait_recv()
        multiply(pos, RELAY, SIB2 + 1)

    def lessen(plane, others):
        for sy in range(8):
            part = in_plane(plane, sy)
            for other in others:
                part = part + diff[1 + other, sy]
            react[plane, sy] -= diffusivity_ref[sy // 4] * part

    def finish(pair):
        for flipped in (0, 1):
            planes = (2 * pair + 1, 2 * pair) if flipped else (2 * pair, 2 * pair + 1)

            @pl.when(flip == flipped)
            def _(planes=planes, block=1 - pair if flipped else pair):
                finish_block(planes, block)

    def finish_block(planes, block):
        @pl.loop(0, MB // 16, unroll=4)
        def _(n):
            rows = pl.ds(pl.multiple_of(16 * n, 16), 16)

            def at(plane, sy):
                return diff[1 + plane, sy, rows, :]

            def in_plane_rows(plane, sy):
                s4 = (sy // 4) * 4
                center = at(plane, sy)
                lap = at(plane, s4 + (sy + 1) % 4) + at(plane, s4 + (sy + 3) % 4)
                lap = lap + (pltpu.roll(center, 1, 1) + pltpu.roll(center, 127, 1))
                return lap - 6.0 * center

            for s in range(2):
                lines = []
                for plane in planes:
                    for sy in range(4 * s, 4 * s + 4):
                        if plane == 0:
                            part = at(1, sy) + halo[0, sy, rows, :].astype(jnp.float32)
                        elif plane == 1:
                            part = at(2, sy)
                        elif plane == 2:
                            part = in_plane_rows(2, sy) + (at(1, sy) + at(3, sy))
                        else:
                            part = at(2, sy) + halo[1, sy, rows, :].astype(jnp.float32)
                        lines.append(diffusivity_ref[s] * part - react[plane, sy, rows, :])
                out_ref[rows, pl.ds(8 * (2 * s + block), 8), :] = jnp.swapaxes(
                    jnp.stack(lines, axis=0), 0, 1
                )

    take_cross(0)
    take_cross(1)
    back[0].wait_recv()
    across[2].start()
    sib.wait_recv()
    across[0].wait_recv()
    multiply(0, OWN, RELAY)
    take_relay(0)

    @pl.when(first)
    def _():
        pl.semaphore_wait(barrier, 2)
        for dy in (1, 2, 3):
            signal(slabs_sem, device(dy, h, c))

    late(0)
    take_cross(2)

    @pl.when(jnp.logical_not(first))
    def _():
        pl.semaphore_wait(slabs_sem, 1)

    halo_up.start()
    across[1].wait_recv()
    multiply(1, OWN, RELAY)
    back[1].wait_recv()
    across[3].start()
    take_cross(3)
    take_relay(1)
    lessen(3, ())
    late(1)
    halo_down.start()
    lessen(0, ())
    across[2].wait_recv()
    multiply(2, OWN, RELAY)
    take_relay(2)
    late(2)
    lessen(1, (0,))
    across[3].wait_recv()
    multiply(3, OWN, RELAY)
    take_relay(3)
    late(3)
    halo_down.wait_recv()
    finish(0)
    halo_up.wait_recv()
    finish(1)

    for copy in (*cross, *relay, *back, *across, sib, *sib_cross, halo_up, halo_down):
        copy.wait_send()


def last_kernel(rate_ref, held_ref, rate_hbm, next_hbm, after, rate_sem, next_sem):
    leave = pltpu.make_async_copy(rate_ref, rate_hbm, rate_sem)
    leave.start()
    size = MB // 2
    copies = []
    for n in range(2):
        rows = pl.ds(n * size, size)
        after[rows] = (held_ref[rows] + half_step * rate_ref[rows]).astype(jnp.bfloat16)
        copies.append(pltpu.make_async_copy(after.at[rows], next_hbm.at[rows], next_sem.at[n]))
        copies[-1].start()
    for copy in copies:
        copy.wait()
    leave.wait()


def shards(
    section_field,
    base_field,
    prev_rate,
    block_list,
    coupling,
    diffusivity,
    reaction_fields,
    species_mix,
):
    rows, species, planes, depth, width = section_field.shape
    flat = rows * species * planes * depth
    lines = species * depth
    in_hbm = pl.BlockSpec(memory_space=pltpu.HBM)
    in_vmem = pl.BlockSpec(memory_space=pltpu.VMEM)
    rate, held = pl.pallas_call(
        kernel,
        name="galerkin",
        out_shape=(
            pltpu.VMEM((rows, STRIDE, width), jnp.float32),
            pltpu.VMEM((rows, STRIDE, width), jnp.float32),
        ),
        in_specs=[in_hbm] * 8,
        out_specs=(in_vmem, in_vmem),
        scratch_shapes=[
            pltpu.SMEM(block_list.shape, block_list.dtype),
            pltpu.SMEM(diffusivity.shape, diffusivity.dtype),
            pltpu.SMEM(species_mix.shape, species_mix.dtype),
            pltpu.VMEM((rows, STRIDE, width), jnp.bfloat16),
            pltpu.VMEM((flat, width), jnp.bfloat16),
            pltpu.VMEM((flat, width), jnp.float32),
            pltpu.VMEM((NNZ, TERMS, MB, MB), jnp.bfloat16),
            pltpu.VMEM((K * planes * depth, width), jnp.bfloat16),
            pltpu.VMEM((K * planes * depth, width), jnp.float32),
            pltpu.VMEM((6, planes, lines, MB, width), jnp.bfloat16),
            pltpu.VMEM((2, lines, MB, width), jnp.bfloat16),
            pltpu.VMEM((TERMS * MB, 6 * MB), jnp.bfloat16),
            pltpu.VMEM((planes + 2, lines, MB, width), jnp.float32),
            pltpu.VMEM((planes, lines, MB, width), jnp.float32),
            pltpu.VMEM((2, lines, MB, width), jnp.bfloat16),
            pltpu.VMEM((2, lines, MB, width), jnp.bfloat16),
            pltpu.SemaphoreType.DMA((flat // PIECE,)),
            pltpu.SemaphoreType.DMA((7,)),
            pltpu.SemaphoreType.DMA((9, 4)),
            pltpu.SemaphoreType.DMA((9, 4)),
            pltpu.SemaphoreType.REGULAR,
            pltpu.SemaphoreType.REGULAR,
            pltpu.SemaphoreType.REGULAR,
        ],
        compiler_params=pltpu.CompilerParams(
            collective_id=0, has_side_effects=True, vmem_limit_bytes=57 * 1024 * 1024
        ),
        cost_estimate=pl.CostEstimate(
            flops=2 * TERMS * 6 * MB * MB * species * planes * depth * width,
            bytes_accessed=2**21,
            transcendentals=0,
        ),
    )(
        section_field.reshape(flat, width),
        coupling.reshape(NNZ, TERMS, MB, MB),
        reaction_fields.reshape(K * planes * depth, width),
        block_list,
        diffusivity,
        species_mix,
        base_field.reshape(rows, STRIDE, width),
        prev_rate.reshape(rows, STRIDE, width),
    )
    rate, next_field = pl.pallas_call(
        last_kernel,
        name="next_section",
        out_shape=(
            jax.ShapeDtypeStruct((rows, STRIDE, width), jnp.float32),
            jax.ShapeDtypeStruct((rows, STRIDE, width), jnp.bfloat16),
        ),
        in_specs=[in_vmem] * 2,
        out_specs=[in_hbm] * 2,
        scratch_shapes=[
            pltpu.VMEM((rows, STRIDE, width), jnp.bfloat16),
            pltpu.SemaphoreType.DMA,
            pltpu.SemaphoreType.DMA((2,)),
        ],
        compiler_params=pltpu.CompilerParams(vmem_limit_bytes=16 * 1024 * 1024),
    )(rate, held)
    return (rate.reshape(section_field.shape), next_field.reshape(section_field.shape))


def solution(mesh):
    placed = (
        P("mode", None, "gx", None, None),
        P("mode", None, "gx", None, None),
        P("mode", None, "gx", None, None),
        P("mode", None),
        P("mode", None, None, None, None),
        P(),
        P(None, "gx", None, None),
        P(),
    )
    return jax.shard_map(
        shards,
        mesh=mesh,
        in_specs=placed,
        out_specs=(P("mode", None, "gx", None, None), P("mode", None, "gx", None, None)),
        check_vma=False,
    )
```

```python
import jax
import jax.numpy as jnp
from jax import lax
from jax.sharding import PartitionSpec as P
import jax.experimental.pallas as pl
import jax.experimental.pallas.tpu as pltpu

MB = 64
NBLK = 16
K = 4
TERMS = 1 + K
NNZ = 5
MESH = pl.DeviceIdType.MESH

half_step = 0.25

OWN, SIB, ACROSS, CROSS, RELAY, SIB2 = range(6)
TRANSIT, HALO_LO, HALO_HI = 6, 7, 8
PLANES = (3, 0, 1, 2)
PIECE = 1024
STRIDE = 32


def kernel(
    section_hbm,
    coupling_hbm,
    fields_hbm,
    list_hbm,
    diffusivity_hbm,
    mix_hbm,
    base_hbm,
    prev_hbm,
    out_ref,
    held_ref,
    list_ref,
    diffusivity_ref,
    mix_ref,
    base,
    native,
    wide,
    couple,
    fields_in,
    fields,
    blocks,
    transit,
    weights,
    diff,
    react,
    edge,
    halo,
    own_sem,
    local_sem,
    send_sem,
    recv_sem,
    ready_sem,
    gather_sem,
    slabs_sem,
):
    g = lax.axis_index("gx")
    i = lax.axis_index("mode")
    y = i // 4
    h = lax.rem(i // 2, 2)
    c = lax.rem(i, 2)
    step = 1 - 2 * h

    def device(dy, hh, cc):
        return (g, lax.rem(y + dy + 4, 4) * 4 + hh * 2 + cc)

    at_cross = device(0, 1 - h, c)
    at_relay = device(step, h, c)
    at_back = device(-step, h, c)
    at_across = device(2, h, c)
    at_sib = device(0, h, 1 - c)
    flip = 1 - lax.rem(g, 2)
    at_up = (lax.rem(g + 17 - 2 * flip, 16), i)
    at_down = (lax.rem(g + 15 + 2 * flip, 16), i)

    def plane_of(plane):
        return plane + flip * (3 - 2 * plane)

    def signal(sem, peer):
        pl.semaphore_signal(sem, inc=1, device_id=peer, device_id_type=MESH)

    pieces = [pl.ds(n * PIECE, PIECE) for n in range(section_hbm.shape[0] // PIECE)]
    own = [
        pltpu.make_async_copy(section_hbm.at[rows], native.at[rows], own_sem.at[n])
        for n, rows in enumerate(pieces)
    ]
    for copy in own:
        copy.start()
    loads = [
        pltpu.make_async_copy(source, target, local_sem.at[n])
        for n, (source, target) in enumerate(
            (
                (coupling_hbm, couple),
                (fields_hbm, fields_in),
                (list_hbm, list_ref),
                (diffusivity_hbm, diffusivity_ref),
                (mix_hbm, mix_ref),
                (base_hbm, base),
                (prev_hbm, held_ref),
            )
        )
    ]

    first = y == 0
    second = y == 1
    barrier = pltpu.get_barrier_semaphore()

    @pl.when(jnp.logical_not(first))
    def _():
        signal(barrier, at_cross)
        signal(barrier, at_sib)

    for dy in (1, 2, 3):

        @pl.when(lax.rem(y + dy, 4) != 0)
        def _(dy=dy):
            signal(barrier, device(dy, h, c))

    @pl.when(first)
    def _():
        signal(barrier, device(1, 1 - h, c))
        signal(barrier, device(1, h, 1 - c))

    for copy in loads:
        copy.start()

    for copy, rows in zip(own, pieces):
        copy.wait()
        wide[rows, :] = native[rows, :].astype(jnp.float32)

    def arrange(pos):
        for sy in range(8):
            start = (sy // 4) * 16 + plane_of(PLANES[pos]) * 4 + sy % 4
            blocks[OWN, pos, sy] = wide[pl.ds(start, MB, stride=STRIDE), :].astype(jnp.bfloat16)

    arrange(0)
    arrange(1)

    @pl.when(second)
    def _():
        pl.semaphore_wait(barrier, 7)
        signal(ready_sem, device(3, h, c))

    @pl.when(y > 1)
    def _():
        pl.semaphore_wait(barrier, 5)
        signal(gather_sem, device(4 - y, h, c))

    @pl.when(first)
    def _():
        pl.semaphore_wait(ready_sem, 1)

    def send(kind, part, source, target, peer):
        return pltpu.make_async_remote_copy(
            src_ref=source,
            dst_ref=target,
            send_sem=send_sem.at[kind, part],
            recv_sem=recv_sem.at[kind, part],
            device_id=peer,
            device_id_type=MESH,
        )

    def block_send(source, target, pos, peer):
        return send(target, pos, blocks.at[source, pos], blocks.at[target, pos], peer)

    every = range(4)
    cross = [block_send(OWN, CROSS, p, at_cross) for p in every]
    relay = [block_send(CROSS, RELAY, p, at_relay) for p in every]
    back = [
        send(TRANSIT, p, blocks.at[OWN, p], transit.at[p - 2], at_back) for p in (2, 3)
    ]
    across = [block_send(OWN, ACROSS, p, at_across) for p in (0, 1)] + [
        send(ACROSS, p, transit.at[p - 2], blocks.at[ACROSS, p], at_back) for p in (2, 3)
    ]
    sib = send(SIB, 0, blocks.at[OWN], blocks.at[SIB], at_sib)
    sib_cross = [block_send(CROSS, SIB2, p, at_sib) for p in every]
    sib_relay = [block_send(RELAY, SIB2, p, at_sib) for p in every]
    halo_up = send(HALO_HI, 0, edge.at[0], halo.at[1], at_up)
    halo_down = send(HALO_LO, 0, edge.at[1], halo.at[0], at_down)

    cross[0].start()
    across[0].start()
    cross[1].start()
    across[1].start()
    arrange(2)
    back[0].start()
    arrange(3)
    back[1].start()
    cross[2].start()
    cross[3].start()
    sib.start()

    @pl.when(first)
    def _():
        pl.semaphore_wait(gather_sem, 2)
        signal(barrier, at_up)
        signal(barrier, at_down)

    for copy in loads:
        copy.wait()
    fields[...] = fields_in[...].astype(jnp.float32)

    def chosen(target):
        target = lax.rem(target + NBLK, NBLK)
        total = None
        for n in range(1, NNZ - 1):
            keep = (list_ref[0, n] == target).astype(jnp.float32)
            term = keep * couple[n].astype(jnp.float32)
            total = term if total is None else total + term
        return total

    def side_by_side(first, second):
        pair = jnp.concatenate([first, second], axis=-1)
        return pair.reshape(TERMS * MB, 2 * MB).astype(jnp.bfloat16)

    weights[:, 0:128] = side_by_side(couple[0].astype(jnp.float32), chosen(i + 1 - 2 * c))
    weights[:, 128:256] = side_by_side(
        couple[NNZ - 1].astype(jnp.float32), chosen(i + 2 - 4 * h)
    )
    weights[:, 256:384] = side_by_side(chosen(i - 2 + 4 * h), chosen(i - 1 + 2 * c))

    @pl.loop(0, 8)
    def _(n):
        rows = pl.ds(n * 8, 8)
        held_ref[rows] = base[rows].astype(jnp.float32) + half_step * held_ref[rows]

    def multiply(pos, first, last):
        plane = PLANES[pos]
        fresh = first == OWN

        @pl.loop(0, 4, unroll=4)
        def _(n):
            sy = n * 2
            s = n // 2
            depth = (last - first) * MB
            sides = [blocks[first:last, pos, sy + k].reshape(depth, 128) for k in (0, 1)]
            result = jnp.dot(
                weights[:, first * MB : last * MB],
                jnp.concatenate(sides, axis=1),
                preferred_element_type=jnp.float32,
            )
            for k in (0, 1):
                columns = slice(128 * k, 128 * (k + 1))
                term_d = result[0:MB, columns]
                yy = lax.rem(sy, 4) + k
                row = plane_of(plane) * 4 + yy
                term_r = fields[pl.ds(row, 1), :] * result[MB : 2 * MB, columns]
                for t in range(1, K):
                    term_r = term_r + fields[pl.ds(16 * t + row, 1), :] * result[
                        (1 + t) * MB : (2 + t) * MB, columns
                    ]
                if fresh:
                    mixed = mix_ref[s, 0] * blocks[OWN, pos, yy].astype(jnp.float32)
                    mixed = mixed + mix_ref[s, 1] * blocks[OWN, pos, 4 + yy].astype(jnp.float32)
                    diff[1 + plane, sy + k] = term_d
                    react[plane, sy + k] = term_r - mixed
                else:
                    total = diff[1 + plane, sy + k] + term_d
                    diff[1 + plane, sy + k] = total
                    react[plane, sy + k] += term_r
                    if pos < 2:
                        edge[pos, sy + k] = total.astype(jnp.bfloat16)

    def in_plane(plane, sy):
        s4 = (sy // 4) * 4
        center = diff[1 + plane, sy]
        lap = diff[1 + plane, s4 + (sy + 1) % 4] + diff[1 + plane, s4 + (sy + 3) % 4]
        lap = lap + (pltpu.roll(center, 1, 1) + pltpu.roll(center, 127, 1))
        return lap - 6.0 * center

    def pass_on(copies, yes, p):
        @pl.when(yes)
        def _():
            copies[p].start()

    def take_cross(p):
        cross[p].wait_recv()
        relay[p].start()
        pass_on(sib_cross, c == h, p)

    def take_relay(p):
        relay[p].wait_recv()
        pass_on(sib_relay, c != h, p)

    def late(pos):
        sib_cross[pos].wait_recv()
        multiply(pos, RELAY, SIB2 + 1)

    def lessen(plane, others):
        for sy in range(8):
            part = in_plane(plane, sy)
            for other in others:
                part = part + diff[1 + other, sy]
            react[plane, sy] -= diffusivity_ref[sy // 4] * part

    def finish(pair):
        for flipped in (0, 1):
            planes = (2 * pair + 1, 2 * pair) if flipped else (2 * pair, 2 * pair + 1)

            @pl.when(flip == flipped)
            def _(planes=planes, block=1 - pair if flipped else pair):
                finish_block(planes, block)

    def finish_block(planes, block):
        @pl.loop(0, MB // 16, unroll=4)
        def _(n):
            rows = pl.ds(pl.multiple_of(16 * n, 16), 16)

            def at(plane, sy):
                return diff[1 + plane, sy, rows, :]

            def in_plane_rows(plane, sy):
                s4 = (sy // 4) * 4
                center = at(plane, sy)
                lap = at(plane, s4 + (sy + 1) % 4) + at(plane, s4 + (sy + 3) % 4)
                lap = lap + (pltpu.roll(center, 1, 1) + pltpu.roll(center, 127, 1))
                return lap - 6.0 * center

            for s in range(2):
                lines = []
                for plane in planes:
                    for sy in range(4 * s, 4 * s + 4):
                        if plane == 0:
                            part = at(1, sy) + halo[0, sy, rows, :].astype(jnp.float32)
                        elif plane == 1:
                            part = at(2, sy)
                        elif plane == 2:
                            part = in_plane_rows(2, sy) + (at(1, sy) + at(3, sy))
                        else:
                            part = at(2, sy) + halo[1, sy, rows, :].astype(jnp.float32)
                        lines.append(diffusivity_ref[s] * part - react[plane, sy, rows, :])
                out_ref[rows, pl.ds(8 * (2 * s + block), 8), :] = jnp.swapaxes(
                    jnp.stack(lines, axis=0), 0, 1
                )

    take_cross(0)
    take_cross(1)
    back[0].wait_recv()
    across[2].start()
    sib.wait_recv()
    across[0].wait_recv()
    multiply(0, OWN, RELAY)
    take_relay(0)

    @pl.when(first)
    def _():
        pl.semaphore_wait(barrier, 2)
        for dy in (1, 2, 3):
            signal(slabs_sem, device(dy, h, c))

    late(0)

    @pl.when(jnp.logical_not(first))
    def _():
        pl.semaphore_wait(slabs_sem, 1)

    halo_up.start()
    take_cross(2)
    across[1].wait_recv()
    multiply(1, OWN, RELAY)
    back[1].wait_recv()
    across[3].start()
    take_cross(3)
    take_relay(1)
    lessen(3, ())
    late(1)
    halo_down.start()
    lessen(0, ())
    across[2].wait_recv()
    multiply(2, OWN, RELAY)
    take_relay(2)
    late(2)
    lessen(1, (0,))
    across[3].wait_recv()
    multiply(3, OWN, RELAY)
    take_relay(3)
    late(3)
    halo_down.wait_recv()
    finish(0)
    halo_up.wait_recv()
    finish(1)

    for copy in (*cross, *relay, *back, *across, sib, *sib_cross, halo_up, halo_down):
        copy.wait_send()


def last_kernel(rate_ref, held_ref, rate_hbm, next_hbm, after, rate_sem, next_sem):
    leave = pltpu.make_async_copy(rate_ref, rate_hbm, rate_sem)
    leave.start()
    size = MB // 2
    copies = []
    for n in range(2):
        rows = pl.ds(n * size, size)
        after[rows] = (held_ref[rows] + half_step * rate_ref[rows]).astype(jnp.bfloat16)
        copies.append(pltpu.make_async_copy(after.at[rows], next_hbm.at[rows], next_sem.at[n]))
        copies[-1].start()
    for copy in copies:
        copy.wait()
    leave.wait()


def shards(
    section_field,
    base_field,
    prev_rate,
    block_list,
    coupling,
    diffusivity,
    reaction_fields,
    species_mix,
):
    rows, species, planes, depth, width = section_field.shape
    flat = rows * species * planes * depth
    lines = species * depth
    in_hbm = pl.BlockSpec(memory_space=pltpu.HBM)
    in_vmem = pl.BlockSpec(memory_space=pltpu.VMEM)
    rate, held = pl.pallas_call(
        kernel,
        name="galerkin",
        out_shape=(
            pltpu.VMEM((rows, STRIDE, width), jnp.float32),
            pltpu.VMEM((rows, STRIDE, width), jnp.float32),
        ),
        in_specs=[in_hbm] * 8,
        out_specs=(in_vmem, in_vmem),
        scratch_shapes=[
            pltpu.SMEM(block_list.shape, block_list.dtype),
            pltpu.SMEM(diffusivity.shape, diffusivity.dtype),
            pltpu.SMEM(species_mix.shape, species_mix.dtype),
            pltpu.VMEM((rows, STRIDE, width), jnp.bfloat16),
            pltpu.VMEM((flat, width), jnp.bfloat16),
            pltpu.VMEM((flat, width), jnp.float32),
            pltpu.VMEM((NNZ, TERMS, MB, MB), jnp.bfloat16),
            pltpu.VMEM((K * planes * depth, width), jnp.bfloat16),
            pltpu.VMEM((K * planes * depth, width), jnp.float32),
            pltpu.VMEM((6, planes, lines, MB, width), jnp.bfloat16),
            pltpu.VMEM((2, lines, MB, width), jnp.bfloat16),
            pltpu.VMEM((TERMS * MB, 6 * MB), jnp.bfloat16),
            pltpu.VMEM((planes + 2, lines, MB, width), jnp.float32),
            pltpu.VMEM((planes, lines, MB, width), jnp.float32),
            pltpu.VMEM((2, lines, MB, width), jnp.bfloat16),
            pltpu.VMEM((2, lines, MB, width), jnp.bfloat16),
            pltpu.SemaphoreType.DMA((flat // PIECE,)),
            pltpu.SemaphoreType.DMA((7,)),
            pltpu.SemaphoreType.DMA((9, 4)),
            pltpu.SemaphoreType.DMA((9, 4)),
            pltpu.SemaphoreType.REGULAR,
            pltpu.SemaphoreType.REGULAR,
            pltpu.SemaphoreType.REGULAR,
        ],
        compiler_params=pltpu.CompilerParams(
            collective_id=0, has_side_effects=True, vmem_limit_bytes=57 * 1024 * 1024
        ),
        cost_estimate=pl.CostEstimate(
            flops=2 * TERMS * 6 * MB * MB * species * planes * depth * width,
            bytes_accessed=2**21,
            transcendentals=0,
        ),
    )(
        section_field.reshape(flat, width),
        coupling.reshape(NNZ, TERMS, MB, MB),
        reaction_fields.reshape(K * planes * depth, width),
        block_list,
        diffusivity,
        species_mix,
        base_field.reshape(rows, STRIDE, width),
        prev_rate.reshape(rows, STRIDE, width),
    )
    rate, next_field = pl.pallas_call(
        last_kernel,
        name="next_section",
        out_shape=(
            jax.ShapeDtypeStruct((rows, STRIDE, width), jnp.float32),
            jax.ShapeDtypeStruct((rows, STRIDE, width), jnp.bfloat16),
        ),
        in_specs=[in_vmem] * 2,
        out_specs=[in_hbm] * 2,
        scratch_shapes=[
            pltpu.VMEM((rows, STRIDE, width), jnp.bfloat16),
            pltpu.SemaphoreType.DMA,
            pltpu.SemaphoreType.DMA((2,)),
        ],
        compiler_params=pltpu.CompilerParams(vmem_limit_bytes=16 * 1024 * 1024),
    )(rate, held)
    return (rate.reshape(section_field.shape), next_field.reshape(section_field.shape))


def solution(mesh):
    placed = (
        P("mode", None, "gx", None, None),
        P("mode", None, "gx", None, None),
        P("mode", None, "gx", None, None),
        P("mode", None),
        P("mode", None, None, None, None),
        P(),
        P(None, "gx", None, None),
        P(),
    )
    return jax.shard_map(
        shards,
        mesh=mesh,
        in_specs=placed,
        out_specs=(P("mode", None, "gx", None, None), P("mode", None, "gx", None, None)),
        check_vma=False,
    )
```
